32 devices in a mesh: req: 2 (over x), wide: 16 (over z, y, core).
Axes of the slice: x: 2, y: 2, z: 4, core: 2. Of those that a mesh axis runs over, the one named last changes fastest.
Arguments:
- tokens: bfloat16 [256, 7168], P(('req', 'wide')), may hold values from -6 to 6
- attn_gain: bfloat16 [7168], replicated, may hold values from 0.099609375 to 1.8984375
- qkv_weight: bfloat16 [7168, 3, 7168], P(None, None, 'wide'), may hold values from -0.122756126 to 0.122756126
- adapter_down: bfloat16 [7168, 384], P('wide'), may hold values from -0.0625 to 0.0625
- adapter_up: bfloat16 [3, 128, 7168], P(None, None, 'wide'), may hold values from -0.5 to 0.5
- out_weight: bfloat16 [7168, 3584], P('wide'), may hold values from -0.0625 to 0.0625
- mlp_gain: bfloat16 [3584], replicated, may hold values from 0.099609375 to 1.8984375
- gate_up: bfloat16 [2, 14336, 3584], P(None, ('req', 'wide')), may hold values from -0.09375 to 0.09375
- down_weight: bfloat16 [14336, 3584], P(('req', 'wide')), may hold values from -0.046875 to 0.046875
- key_cache: bfloat16 [2, 4096, 7168], P('req', 'wide'), may hold values from -12 to 12
- value_cache: bfloat16 [2, 4096, 7168], P('req', 'wide'), may hold values from -6 to 6
- cache_lengths: int32 [2], P('req'), may hold values from 65 to 4096, as said below
- slot_mask: int32 [2, 4096], P('req', 'wide'), may hold values 0 or 1
- span_counts: int32 [2], P('req'), may hold values from 32 to 128, as said below
Outputs:
- hidden_out: bfloat16 [256, 3584], P(('req', 'wide'))
- attention: bfloat16 [256, 7168], P('req', 'wide')
- new_keys: bfloat16 [256, 7168], P('req', 'wide')
- new_values: bfloat16 [256, 7168], P('req', 'wide')
The draws below stay inside these ranges and needn't reach their ends.
Inputs may be any that keep to these rules, and one draw needn't show every extreme that they name: `cache_lengths`: the longest request has exactly 4096 filled positions in every draw. `span_counts`: some request fills all 128 slots in every draw.
All inputs are finite; a program needn't handle non-finite values. No bound on the sum of `slot_mask` on one device may be relied on, other than what follows from the above.
Results may differ from the reference program's by a relative error of at most 0.024.
Values may be sent and summed in bfloat16 or wider, within the bound.
A program may use at most 512 MiB of HBM per device.

```python
import jax
import jax.numpy as jnp
from jax import lax

D = 7168
HID = 3584
HEADS = 32
HD = 224
RANK = 128
FF = 14336
SPAN = 128
REQS = 2
CAP = 4096
TOKENS = 256


def request_lengths(key):
    first_key, second_key, third_key = jax.random.split(jax.random.fold_in(key, 3), 3)
    shifts = jax.random.randint(first_key, (REQS,), 0, 6)
    ceiling = jnp.right_shift(jnp.full((REQS,), CAP, jnp.int32), shifts.astype(jnp.int32))
    reduction = jax.random.randint(second_key, (REQS,), 0, ceiling // 2)
    lengths = ceiling - reduction
    longest = jax.random.randint(third_key, (), 0, REQS)
    return jnp.where(jnp.arange(REQS) == longest, CAP, lengths).astype(jnp.int32)


def draw_cache_lengths(key, part):
    return request_lengths(key)


def draw_span_counts(key, part):
    first_key, second_key = jax.random.split(jax.random.fold_in(key, 7), 2)
    counts = jax.random.randint(first_key, (REQS,), SPAN // 4, SPAN + 1)
    fullest = jax.random.randint(second_key, (), 0, REQS)
    return jnp.where(jnp.arange(REQS) == fullest, SPAN, counts).astype(jnp.int32)


def draw_tokens(key, part):
    noise_key = jax.random.fold_in(jax.random.fold_in(key, 17), 0)
    values = jax.random.normal(noise_key, (TOKENS, D), jnp.float32)
    return jnp.clip(values, -6.0, 6.0).astype(jnp.bfloat16)


def draw_qkv_weight(key, part):
    sigma = (D // 3) ** (-0.5)
    values = sigma * jax.random.normal(jax.random.fold_in(key, 19), (D, 3, D), jnp.float32)
    return jnp.clip(values, -6.0 * sigma, 6.0 * sigma).astype(jnp.bfloat16)


def draw_key_cache(key, part):
    values = 2.0 * jax.random.normal(jax.random.fold_in(key, 23), (REQS, CAP, D), jnp.float32)
    values = jnp.clip(values, -12.0, 12.0)
    return values.astype(jnp.bfloat16)


def touch_ends(values, own_key, low, top_value):
    dims = values.shape
    place = [jax.random.randint(jax.random.fold_in(own_key, axis), (), 0, dims[axis]) for axis in range(len(dims))]
    values = values.at[tuple(place)].set(low)
    longest = dims.index(max(dims))
    place[longest] = (place[longest] + 1) % dims[longest]
    return values.at[tuple(place)].set(top_value)


def level_of(stream_key, shape, pieces, smallest, top_value):
    def one(axis_at, parts):
        steps = jax.random.uniform(jax.random.fold_in(jax.random.fold_in(stream_key, 6), axis_at), (parts,), jnp.float32, smallest / len(pieces), top_value / len(pieces))
        return jnp.repeat(jnp.exp(steps), shape[axis_at] // parts).reshape((-1,) + (1,) * (len(shape) - axis_at - 1))

    factor_of = one(*pieces[0])
    for cut in pieces[1:]:
        factor_of = factor_of * one(*cut)
    return factor_of


def bell_draw(own_key, extent, spread, reach, cuts=(), held_as=jnp.bfloat16):
    array = spread * jax.random.normal(own_key, extent, jnp.float32)
    if cuts:
        array = array * level_of(own_key, extent, cuts, -0.22, 0.18)
    return jnp.clip(array, -reach, reach).astype(held_as)


def setup_inputs(seed: int = 0) -> dict:
    splits = jax.random.split(jax.random.key(seed), 15)
    tokens = draw_tokens(jax.random.fold_in(splits[14], 71), 0)
    attn_gain = jnp.clip(1.0 + 0.18 * jax.random.normal(splits[1], (D,), jnp.float32), 0.099609375, 1.8984375).astype(jnp.bfloat16)
    qkv_weight = draw_qkv_weight(jax.random.fold_in(splits[14], 71), 0)
    adapter_down = bell_draw(splits[3], (D, 3 * RANK), D ** -0.5, 0.0625, ((0, 16),))
    adapter_up = bell_draw(splits[4], (3, RANK, D), RANK ** -0.5, 0.5, ((2, 16),))
    out_weight = bell_draw(splits[5], (D, HID), D ** -0.5, 0.0625, ((0, 16),))
    mlp_gain = jnp.clip(1.0 + 0.18 * jax.random.normal(splits[6], (HID,), jnp.float32), 0.099609375, 1.8984375).astype(jnp.bfloat16)
    gate_up = bell_draw(splits[7], (2, FF, HID), HID ** -0.5, 0.09375, ((1, 32),))
    down_weight = bell_draw(splits[8], (FF, HID), FF ** -0.5, 0.046875, ((0, 32),))
    key_cache = draw_key_cache(jax.random.fold_in(splits[14], 71), 0)
    value_cache = bell_draw(splits[10], (REQS, CAP, D), 1.0, 6.0, ((0, 2), (1, 16)))
    cache_lengths = draw_cache_lengths(jax.random.fold_in(splits[14], 71), 0)
    slot_mask = touch_ends((jax.random.randint(splits[12], (REQS, CAP), 0, 8) < 7).astype(jnp.int32), jax.random.fold_in(splits[12], 1), 0, 1)
    span_counts = draw_span_counts(jax.random.fold_in(splits[14], 71), 0)
    return dict(tokens=tokens, attn_gain=attn_gain, qkv_weight=qkv_weight, adapter_down=adapter_down, adapter_up=adapter_up, out_weight=out_weight, mlp_gain=mlp_gain, gate_up=gate_up, down_weight=down_weight, key_cache=key_cache, value_cache=value_cache, cache_lengths=cache_lengths, slot_mask=slot_mask, span_counts=span_counts)


EPSILON = 1e-05
NEG_LARGE = -1e+30

def rms_scale(values, gains):
    widened = values.astype(jnp.float32)
    meansq = lax.optimization_barrier(jnp.mean(widened * widened, axis=-1, keepdims=True))
    return (widened * lax.rsqrt(meansq + EPSILON) * gains.astype(jnp.float32)).astype(jnp.bfloat16)

def attend(inputs):
    query_rows, keys_old, values_old, keys_new, values_new, length, filled, span_count = inputs
    score_scale = HD ** (-0.5)
    query_heads = query_rows.reshape(SPAN, HEADS, HD).astype(jnp.float32)
    all_keys = jnp.concatenate([keys_old, keys_new], 0).reshape(CAP + SPAN, HEADS, HD).astype(jnp.float32)
    all_values = jnp.concatenate([values_old, values_new], 0).reshape(CAP + SPAN, HEADS, HD).astype(jnp.float32)
    scores = jnp.einsum('qhd,khd->hqk', query_heads, all_keys) * score_scale
    positions = jnp.arange(CAP)
    cache_ok = (positions < length) & (filled == 1)
    query_pos = jnp.arange(SPAN)[:, None]
    key_pos = jnp.arange(SPAN)[None, :]
    span_ok = (key_pos <= query_pos) & ((key_pos < span_count) | (key_pos == query_pos))
    allowed = jnp.concatenate([jnp.broadcast_to(cache_ok[None, :], (SPAN, CAP)), span_ok], 1)
    scores = jnp.where(allowed[None], scores, NEG_LARGE)
    highest = lax.optimization_barrier(jnp.max(scores, axis=-1, keepdims=True))
    weights = jnp.where(allowed[None], jnp.exp(scores - highest), 0.0)
    totals = lax.optimization_barrier(jnp.sum(weights, axis=-1))
    rounded = weights.astype(jnp.bfloat16).astype(jnp.float32)
    mixed = jnp.einsum('hqk,khd->qhd', rounded, all_values)
    result = mixed / jnp.transpose(totals)[:, :, None]
    return result.reshape(SPAN, D).astype(jnp.bfloat16)

def reference(tokens, attn_gain, qkv_weight, adapter_down, adapter_up, out_weight, mlp_gain, gate_up, down_weight, key_cache, value_cache, cache_lengths, slot_mask, span_counts):
    normed = rms_scale(tokens, attn_gain)
    base_part = jnp.dot(normed, qkv_weight.reshape(D, 3 * D), preferred_element_type=jnp.float32).reshape(TOKENS, 3, D)
    lowrank = jnp.dot(normed, adapter_down, preferred_element_type=jnp.float32).astype(jnp.bfloat16)
    adapted = jnp.einsum('tcr,crd->tcd', lowrank.reshape(TOKENS, 3, RANK).astype(jnp.float32), adapter_up.astype(jnp.float32))
    projected = (base_part + adapted).astype(jnp.bfloat16)
    query_all = projected[:, 0]
    new_keys = projected[:, 1]
    new_values = projected[:, 2]
    attention = lax.map(attend, (query_all.reshape(REQS, SPAN, D), key_cache, value_cache, new_keys.reshape(REQS, SPAN, D), new_values.reshape(REQS, SPAN, D), cache_lengths, slot_mask, span_counts))
    attention = attention.reshape(TOKENS, D)
    attn_out = jnp.dot(attention, out_weight, preferred_element_type=jnp.float32)
    normed_mid = rms_scale(attn_out, mlp_gain)
    both = jnp.einsum('td,cfd->ctf', normed_mid.astype(jnp.float32), gate_up.astype(jnp.float32))
    hidden = (jax.nn.silu(both[0]) * both[1]).astype(jnp.bfloat16)
    mlp_out = jnp.dot(hidden, down_weight, preferred_element_type=jnp.float32)
    hidden_out = mlp_out.astype(jnp.bfloat16)
    return (hidden_out, attention, new_keys, new_values)
```

```python
import functools

import jax
import jax.numpy as jnp
from jax import lax
from jax.experimental import pallas as pl
from jax.experimental.pallas import tpu as pltpu
from jax.sharding import PartitionSpec as P

D = 7168
HEADS = 32
HD = 224
RANK = 128
SPAN = 128
GROUP = 4

EPSILON = 1e-05
NEG_LARGE = -1e30
MESH = pl.DeviceIdType.MESH
VMEM_LIMIT = 48 * 1024 * 1024


def rms_scale(values, gains):
    widened = values.astype(jnp.float32)
    meansq = jnp.mean(widened * widened, axis=-1, keepdims=True)
    return (widened * lax.rsqrt(meansq + EPSILON) * gains.astype(jnp.float32)).astype(jnp.bfloat16)


def params(collective_id=None):
    if collective_id is None:
        return pltpu.CompilerParams(vmem_limit_bytes=VMEM_LIMIT)
    return pltpu.CompilerParams(
        collective_id=collective_id, has_side_effects=True, vmem_limit_bytes=VMEM_LIMIT
    )


class Grid:
    def __init__(self, reqs, wide):
        self.wide = wide
        chips = wide // 2
        first = 4 if chips % 4 == 0 else 1
        self.size = dict(r=reqs, a=first, b=chips // first, c=2)

    def place(self):
        me = lax.axis_index("wide")
        b = self.size["b"]
        return dict(
            r=lax.axis_index("req"), a=me // (2 * b), b=(me // 2) % b, c=me % 2
        )

    def moved(self, place, **steps):
        out = dict(place)
        for axis, step in steps.items():
            if step:
                out[axis] = (place[axis] + step) % self.size[axis]
        return out

    def on_wide(self, place):
        return (place["a"] * self.size["b"] + place["b"]) * 2 + place["c"]

    def device(self, place):
        return (place["r"], self.on_wide(place))

    def barrier(self, me, axes):
        sem = pltpu.get_barrier_semaphore()
        count = 0
        for axis in axes:
            for step in range(1, self.size[axis]):
                pl.semaphore_signal(
                    sem,
                    inc=1,
                    device_id=self.device(self.moved(me, **{axis: step})),
                    device_id_type=MESH,
                )
                count += 1
        pl.semaphore_wait(sem, count)


def remote(src, dst, send, recv, device):
    return pltpu.make_async_remote_copy(
        src_ref=src, dst_ref=dst, send_sem=send, recv_sem=recv, device_id=device, device_id_type=MESH
    )


def spread(grid, me, order, x_ref, o_ref, send, recv, local):
    def slot(place):
        at = grid.on_wide(place)
        return place["r"] * grid.wide + at if "r" in order else at

    own = pltpu.make_async_copy(x_ref, o_ref.at[slot(me)], local)
    own.start()
    items = [((0,) * len(order), -1)]
    for k, axis in enumerate(order):
        items += [
            (steps[:k] + (s,) + steps[k + 1 :], k)
            for steps, _ in list(items)
            for s in range(1, grid.size[axis])
        ]
    items.sort(key=lambda item: (sum(1 for s in item[0] if s), item[1]))
    sends = []
    for steps, stage in items:
        place = grid.moved(me, **dict(zip(order, steps)))
        here = o_ref.at[slot(place)]
        if stage >= 0:
            remote(x_ref, here, send.at[0], recv.at[slot(place)], grid.device(me)).wait_recv()
        source = here if stage >= 0 else x_ref
        for k in range(stage + 1, len(order)):
            for s in range(1, grid.size[order[k]]):
                copy = remote(
                    source,
                    here,
                    send.at[len(sends)],
                    recv.at[slot(place)],
                    grid.device(grid.moved(me, **{order[k]: s})),
                )
                copy.start()
                sends.append(copy)
    own.wait()
    for copy in sends:
        copy.wait_send()


def gather_kernel(grid, order, x_ref, o_ref, send, recv, local):
    me = grid.place()
    grid.barrier(me, order)
    spread(grid, me, order, x_ref, o_ref, send, recv, local)


def gather(grid, order, x, collective_id):
    slots = grid.wide * (grid.size["r"] if "r" in order else 1)
    return pl.pallas_call(
        functools.partial(gather_kernel, grid, order),
        out_shape=jax.ShapeDtypeStruct((slots,) + x.shape, x.dtype),
        in_specs=[pl.BlockSpec(memory_space=pltpu.VMEM)],
        out_specs=pl.BlockSpec(memory_space=pltpu.VMEM),
        scratch_shapes=[
            pltpu.SemaphoreType.DMA((slots,)),
            pltpu.SemaphoreType.DMA((slots,)),
            pltpu.SemaphoreType.DMA,
        ],
        compiler_params=params(collective_id),
        name="gather" + str(collective_id),
    )(x)


def lowrank_kernel(grid, p_ref, o_ref, r_ref, t_ref, sems):
    me = lax.axis_index("wide")
    req = lax.axis_index("req")
    n = grid.wide
    barrier = pltpu.get_barrier_semaphore()
    for d in range(1, n):
        pl.semaphore_signal(barrier, inc=1, device_id=(req, (me + d) % n), device_id_type=MESH)
    pl.semaphore_wait(barrier, n - 1)
    first = []
    for d in range(1, n):
        to = (me + d) % n
        copy = remote(p_ref.at[to], r_ref.at[d - 1], sems.at[0, d], sems.at[1, d], (req, to))
        copy.start()
        first.append(copy)
    total = p_ref[me]
    for d, copy in enumerate(first):
        copy.wait_recv()
        total = total + r_ref[d]
    t_ref[...] = total.astype(t_ref.dtype)
    second = []
    for d in range(1, n):
        copy = remote(t_ref, o_ref.at[me], sems.at[2, d], sems.at[3, d], (req, (me + d) % n))
        copy.start()
        second.append(copy)
    o_ref[me] = t_ref[...]
    for d in range(1, n):
        remote(t_ref, o_ref.at[(me + n - d) % n], sems.at[2, d], sems.at[3, d], (req, me)).wait_recv()
    for copy in first + second:
        copy.wait_send()


def lowrank_sum(grid, partial, collective_id):
    n, rows, width = partial.shape
    vmem = pl.BlockSpec(memory_space=pltpu.VMEM)
    return pl.pallas_call(
        functools.partial(lowrank_kernel, grid),
        out_shape=jax.ShapeDtypeStruct(partial.shape, jnp.bfloat16),
        in_specs=[vmem],
        out_specs=vmem,
        scratch_shapes=[
            pltpu.VMEM((n - 1, rows, width), jnp.float32),
            pltpu.VMEM((rows, width), jnp.bfloat16),
            pltpu.SemaphoreType.DMA((4, n)),
        ],
        compiler_params=params(collective_id),
        name="lowrank_sum",
    )(partial)


def add_join(first, second):
    return [x + y for x, y in zip(first, second)]


def softmax_join(first, second):
    num1, st1 = first
    num2, st2 = second
    max1, sum1 = st1[..., :GROUP, :], st1[..., GROUP:, :]
    max2, sum2 = st2[..., :GROUP, :], st2[..., GROUP:, :]
    highest = jnp.maximum(max1, max2)
    f1 = jnp.exp(max1 - highest)
    f2 = jnp.exp(max2 - highest)
    heads = num1.shape[-3]
    num = jnp.stack(
        [
            num1[..., i, :, :] * f1[..., i : i + 1, :] + num2[..., i, :, :] * f2[..., i : i + 1, :]
            for i in range(heads)
        ],
        axis=-3,
    )
    return [num, jnp.concatenate([highest, sum1 * f1 + sum2 * f2], axis=-2)]


def combine_down(grid, me, reqs, join, ps, sc, sems):
    R, A, B = reqs, grid.size["a"], grid.size["b"]
    r, a, b, c = (me["r"] if R > 1 else 0), me["a"], me["b"], me["c"]
    parts = range(len(ps))
    sends = []
    count = [0]

    def push(pairs, device):
        out = []
        for i, (src, dst) in enumerate(pairs):
            k = count[0]
            count[0] += 1
            copy = remote(src, dst, sems.at[0, k], sems.at[1, k], device)
            copy.start()
            out.append(copy)
        sends.extend(out)
        return out

    def arrived(copies):
        for copy in copies:
            copy.wait_recv()

    def wide_values(refs):
        return [ref[...].astype(jnp.float32) for ref in refs]

    others = list(range(1, B)) + [0]
    core = {}
    peer = grid.device(grid.moved(me, c=1))
    for dr in list(range(1, R)) + [0]:
        rr = (r + dr) % R if dr else r
        for db in others:
            bb = (b + db) % B if db else b
            core[dr, db] = push(
                [(ps[i].at[rr, :, bb, 1 - c], sc["r1"][i].at[rr, bb]) for i in parts], peer
            )
    along_r = {}
    for dr in range(1, R):
        rr = (r + dr) % R
        for db in others:
            bb = (b + db) % B if db else b
            arrived(core[dr, db])
            both = join(
                wide_values([ps[i].at[rr, :, bb, c] for i in parts]),
                wide_values([sc["r1"][i].at[rr, bb] for i in parts]),
            )
            for i in parts:
                sc["t1"][i][rr, bb] = both[i].astype(sc["t1"][i].dtype)
            along_r[dr, db] = push(
                [(sc["t1"][i].at[rr, bb], sc["r2"][i].at[dr - 1, bb]) for i in parts],
                grid.device(grid.moved(me, r=dr)),
            )
    along_b = {}
    for db in others:
        bb = (b + db) % B if db else b
        arrived(core[0, db])
        both = join(
            wide_values([ps[i].at[r, :, bb, c] for i in parts]),
            wide_values([sc["r1"][i].at[r, bb] for i in parts]),
        )
        for dr in range(1, R):
            arrived(along_r[dr, db])
            both = join(both, wide_values([sc["r2"][i].at[dr - 1, bb] for i in parts]))
        if db:
            for i in parts:
                sc["t2"][i][bb] = both[i].astype(sc["t2"][i].dtype)
            along_b[db] = push(
                [(sc["t2"][i].at[bb], sc["r3"][i].at[db - 1]) for i in parts],
                grid.device(grid.moved(me, b=db)),
            )
    for db in range(1, B):
        arrived(along_b[db])
        both = join(both, wide_values([sc["r3"][i].at[db - 1] for i in parts]))
    for i in parts:
        sc["own"][i][...] = both[i]
        sc["t3"][i][...] = both[i].astype(sc["t3"][i].dtype)
    along_a = []
    for da in range(1, A):
        aa = (a + da) % A
        along_a.append(
            push(
                [(sc["t3"][i].at[aa], sc["r4"][i].at[da - 1]) for i in parts],
                grid.device(grid.moved(me, a=da)),
            )
        )
    total = [sc["own"][i][a] for i in parts]
    for da in range(1, A):
        arrived(along_a[da - 1])
        total = join(total, wide_values([sc["r4"][i].at[da - 1] for i in parts]))
    return total, sends


SCRATCH = ("r1", "t1", "r2", "t2", "r3", "own", "t3", "r4")


def reduce_scratch(grid, reqs, slabs):
    R, A, B = reqs, grid.size["a"], grid.size["b"]
    lead = dict(
        r1=(R, B, A),
        t1=(R if R > 1 else 1, B if R > 1 else 1, A if R > 1 else 1),
        r2=(R - 1, B, A) if R > 1 else (1, 1, 1),
        t2=(B, A),
        r3=(max(B - 1, 1), A),
        own=(A,),
        t3=(A,),
        r4=(max(A - 1, 1),),
    )
    shapes = []
    for name in SCRATCH:
        for shape, dtype in slabs:
            shapes.append(
                pltpu.VMEM(lead[name] + tuple(shape), jnp.float32 if name == "own" else dtype)
            )
    copies = (R * B + (R - 1) * B + (B - 1) + (A - 1)) * len(slabs)
    shapes.append(pltpu.SemaphoreType.DMA((2, copies)))
    return shapes


def reduce_kernel(grid, reqs, join, parts, *refs):
    ps, outs, rest, sems = refs[:parts], refs[parts : 2 * parts], refs[2 * parts : -1], refs[-1]
    sc = {name: rest[k * parts : (k + 1) * parts] for k, name in enumerate(SCRATCH)}
    me = grid.place()
    grid.barrier(me, ("r", "a", "b", "c") if reqs > 1 else ("a", "b", "c"))
    total, sends = combine_down(grid, me, reqs, join, ps, sc, sems)
    for out, value in zip(outs, total):
        out[...] = value.astype(out.dtype)
    for copy in sends:
        copy.wait_send()


def reduce_scatter(grid, reqs, join, arrays, out_dtypes, collective_id):
    A, B = grid.size["a"], grid.size["b"]
    slabs = [(x.shape[1:], x.dtype) for x in arrays]
    vmem = pl.BlockSpec(memory_space=pltpu.VMEM)
    return pl.pallas_call(
        functools.partial(reduce_kernel, grid, reqs, join, len(arrays)),
        out_shape=[jax.ShapeDtypeStruct(s, t) for (s, _), t in zip(slabs, out_dtypes)],
        in_specs=[vmem] * len(arrays),
        out_specs=[vmem] * len(arrays),
        scratch_shapes=reduce_scratch(grid, reqs, slabs),
        compiler_params=params(collective_id),
        name="reduce" + str(collective_id),
    )(*[x.reshape((reqs, A, B, 2) + x.shape[1:]) for x in arrays])


def cache_kernel(heads, q_ref, k_ref, v_ref, ok_ref, num_ref, st_ref):
    ok = ok_ref[...] > 0.0
    st_ref[...] = jnp.zeros_like(st_ref)
    for i in range(GROUP):
        keys = k_ref[0, :, i * HD : (i + 1) * HD]
        values = v_ref[0, :, i * HD : (i + 1) * HD]
        scores = jnp.dot(keys, q_ref[i], preferred_element_type=jnp.float32) * HD ** (-0.5)
        scores = jnp.where(ok, scores, NEG_LARGE)
        highest = jnp.max(scores, axis=0, keepdims=True)
        weights = jnp.where(ok, jnp.exp(scores - highest), 0.0)
        num = lax.dot_general(
            values,
            weights.astype(jnp.bfloat16),
            (((0,), (0,)), ((), ())),
            preferred_element_type=jnp.float32,
        )
        num_ref[i] = num.astype(jnp.bfloat16)
        slab, row = i // heads, i % heads
        st_ref[slab, row : row + 1, :] = highest
        st_ref[slab, GROUP + row : GROUP + row + 1, :] = jnp.sum(weights, axis=0, keepdims=True)


def cache_attention(heads, query, keys, values, usable):
    block = keys.shape[1]
    cols = GROUP * HD
    kv = pl.BlockSpec((1, block, cols), lambda i: (0, 0, i))
    return pl.pallas_call(
        functools.partial(cache_kernel, heads),
        grid=(HEADS // GROUP,),
        in_specs=[
            pl.BlockSpec((GROUP, HD, SPAN), lambda i: (i, 0, 0)),
            kv,
            kv,
            pl.BlockSpec((block, SPAN), lambda i: (0, 0)),
        ],
        out_specs=[
            pl.BlockSpec((GROUP, HD, SPAN), lambda i: (i, 0, 0)),
            pl.BlockSpec((GROUP // heads, 2 * GROUP, SPAN), lambda i: (i, 0, 0)),
        ],
        out_shape=[
            jax.ShapeDtypeStruct((HEADS, HD, SPAN), jnp.bfloat16),
            jax.ShapeDtypeStruct((HEADS // heads, 2 * GROUP, SPAN), jnp.float32),
        ],
        compiler_params=params(),
        name="cache_attention",
    )(query, keys, values, usable)


def body(
    grid,
    tokens,
    attn_gain,
    qkv_weight,
    adapter_down,
    adapter_up,
    out_weight,
    mlp_gain,
    gate_up,
    down_weight,
    key_cache,
    value_cache,
    cache_lengths,
    slot_mask,
    span_counts,
):
    reqs, wide = grid.size["r"], grid.wide
    rows = tokens.shape[0]
    width = qkv_weight.shape[2]
    heads = width // HD
    wide_index = lax.axis_index("wide")
    normed = rms_scale(tokens, attn_gain)
    shard_rows = gather(grid, ("a", "b", "c"), normed, 0).reshape(SPAN, D)
    sliced = lax.dynamic_slice_in_dim(shard_rows, wide_index * width, width, 1)
    partial_low = jnp.dot(sliced, adapter_down, preferred_element_type=jnp.float32)
    lowrank = lowrank_sum(grid, partial_low.reshape(wide, rows, 3 * RANK), 1)
    base = jnp.dot(shard_rows, qkv_weight.reshape(D, 3 * width), preferred_element_type=jnp.float32)
    adapted = jnp.einsum(
        "tcr,crd->tcd",
        lowrank.reshape(SPAN, 3, RANK),
        adapter_up,
        preferred_element_type=jnp.float32,
    )
    projected = (base.reshape(SPAN, 3, width) + adapted).astype(jnp.bfloat16)
    query_own = projected[:, 0]
    new_keys = projected[:, 1]
    new_values = projected[:, 2]
    query_turned = query_own.T.reshape(heads, HD, SPAN)
    query_all = gather(grid, ("a", "b", "c"), query_turned, 2).reshape(HEADS, HD, SPAN)

    block_len = key_cache.shape[1]
    positions = wide_index * block_len + jnp.arange(block_len)
    usable = ((positions < cache_lengths[0]) & (slot_mask[0] == 1)).astype(jnp.float32)
    usable = jnp.broadcast_to(usable[:, None], (block_len, SPAN))
    num, stats = cache_attention(heads, query_all, key_cache, value_cache, usable)
    cache_num, cache_stats = reduce_scatter(
        grid,
        1,
        softmax_join,
        [num.reshape(wide, heads, HD, SPAN), stats],
        [jnp.float32, jnp.float32],
        3,
    )

    span_count = span_counts[0]
    query_pos = jnp.arange(SPAN)[None, :]
    key_pos = jnp.arange(SPAN)[:, None]
    span_ok = (key_pos <= query_pos) & ((key_pos < span_count) | (key_pos == query_pos))
    own_scores = (
        jnp.einsum(
            "hdq,khd->hkq",
            query_turned,
            new_keys.reshape(SPAN, heads, HD),
            preferred_element_type=jnp.float32,
        )
        * HD ** (-0.5)
    )
    own_scores = jnp.where(span_ok, own_scores, NEG_LARGE)
    own_max = jnp.max(own_scores, axis=1)
    own_weights = jnp.where(span_ok, jnp.exp(own_scores - own_max[:, None]), 0.0)
    own_sum = jnp.sum(own_weights, axis=1)
    own_num = jnp.einsum(
        "hkq,khd->hdq",
        own_weights.astype(jnp.bfloat16),
        new_values.reshape(SPAN, heads, HD),
        preferred_element_type=jnp.float32,
    )
    cache_max, cache_sum = cache_stats[:heads], cache_stats[GROUP : GROUP + heads]
    highest = jnp.maximum(cache_max, own_max)
    cache_factor = jnp.exp(cache_max - highest)
    own_factor = jnp.exp(own_max - highest)
    totals = cache_sum * cache_factor + own_sum * own_factor
    mixed = cache_num * cache_factor[:, None] + own_num * own_factor[:, None]
    attention = (mixed / totals[:, None]).astype(jnp.bfloat16).reshape(width, SPAN).T

    attn_part = jnp.dot(attention, out_weight, preferred_element_type=jnp.float32)
    (attn_out,) = reduce_scatter(
        grid,
        1,
        add_join,
        [attn_part.astype(jnp.bfloat16).reshape(wide, rows, -1)],
        [jnp.float32],
        4,
    )
    normed_mid = rms_scale(attn_out, mlp_gain)
    every_row = gather(grid, ("a", "b", "r", "c"), normed_mid, 5).reshape(reqs * SPAN, -1)
    both = jnp.einsum("td,cfd->ctf", every_row, gate_up, preferred_element_type=jnp.float32)
    hidden = (jax.nn.silu(both[0]) * both[1]).astype(jnp.bfloat16)
    mlp_part = jnp.dot(hidden, down_weight, preferred_element_type=jnp.float32)
    (hidden_out,) = reduce_scatter(
        grid,
        reqs,
        add_join,
        [mlp_part.astype(jnp.bfloat16).reshape(reqs * wide, rows, -1)],
        [jnp.bfloat16],
        6,
    )
    return (hidden_out, attention, new_keys, new_values)


def solution(mesh):
    grid = Grid(mesh.shape["req"], mesh.shape["wide"])
    return jax.shard_map(
        functools.partial(body, grid),
        mesh=mesh,
        in_specs=(
            P(("req", "wide"), None),
            P(),
            P(None, None, "wide"),
            P("wide", None),
            P(None, None, "wide"),
            P("wide", None),
            P(),
            P(None, ("req", "wide"), None),
            P(("req", "wide"), None),
            P("req", "wide", None),
            P("req", "wide", None),
            P("req"),
            P("req", "wide"),
            P("req"),
        ),
        out_specs=(P(("req", "wide"), None), P("req", "wide"), P("req", "wide"), P("req", "wide")),
        check_vma=False,
    )
```

```python
import functools
import math

import jax
import jax.numpy as jnp
from jax import lax
from jax.experimental import pallas as pl
from jax.experimental.pallas import tpu as pltpu
from jax.sharding import PartitionSpec as P

D = 7168
HEADS = 32
HD = 224
RANK = 128
SPAN = 128
GROUP = 4

EPSILON = 1e-05
NEG_LARGE = -1e30
MESH = pl.DeviceIdType.MESH
VMEM_LIMIT = 48 * 1024 * 1024


def rms_scale(values, gains):
    widened = values.astype(jnp.float32)
    meansq = jnp.mean(widened * widened, axis=-1, keepdims=True)
    return (widened * lax.rsqrt(meansq + EPSILON) * gains.astype(jnp.float32)).astype(jnp.bfloat16)


def params(collective_id=None):
    if collective_id is None:
        return pltpu.CompilerParams(vmem_limit_bytes=VMEM_LIMIT)
    return pltpu.CompilerParams(
        collective_id=collective_id, has_side_effects=True, vmem_limit_bytes=VMEM_LIMIT
    )


class Grid:
    def __init__(self, reqs, wide):
        self.wide = wide
        chips = wide // 2
        first = 4 if chips % 4 == 0 else 1
        self.size = dict(r=reqs, a=first, b=chips // first, c=2)

    def place(self):
        me = lax.axis_index("wide")
        b = self.size["b"]
        return dict(
            r=lax.axis_index("req"), a=me // (2 * b), b=(me // 2) % b, c=me % 2
        )

    def moved(self, place, **steps):
        out = dict(place)
        for axis, step in steps.items():
            if step:
                out[axis] = (place[axis] + step) % self.size[axis]
        return out

    def on_wide(self, place):
        return (place["a"] * self.size["b"] + place["b"]) * 2 + place["c"]

    def device(self, place):
        return (place["r"], self.on_wide(place))

    def barrier(self, me, axes):
        sem = pltpu.get_barrier_semaphore()
        count = 0
        for axis in axes:
            for step in range(1, self.size[axis]):
                pl.semaphore_signal(
                    sem,
                    inc=1,
                    device_id=self.device(self.moved(me, **{axis: step})),
                    device_id_type=MESH,
                )
                count += 1
        pl.semaphore_wait(sem, count)


def remote(src, dst, send, recv, device):
    return pltpu.make_async_remote_copy(
        src_ref=src, dst_ref=dst, send_sem=send, recv_sem=recv, device_id=device, device_id_type=MESH
    )


def spread(grid, me, order, x_ref, o_ref, send, recv, local):
    def slot(place):
        at = grid.on_wide(place)
        return place["r"] * grid.wide + at if "r" in order else at

    own = pltpu.make_async_copy(x_ref, o_ref.at[slot(me)], local)
    own.start()
    items = [((0,) * len(order), -1)]
    for k, axis in enumerate(order):
        items += [
            (steps[:k] + (s,) + steps[k + 1 :], k)
            for steps, _ in list(items)
            for s in range(1, grid.size[axis])
        ]
    items.sort(key=lambda item: (sum(1 for s in item[0] if s), item[1]))
    sends = []
    for steps, stage in items:
        place = grid.moved(me, **dict(zip(order, steps)))
        here = o_ref.at[slot(place)]
        if stage >= 0:
            remote(x_ref, here, send.at[0], recv.at[slot(place)], grid.device(me)).wait_recv()
        source = here if stage >= 0 else x_ref
        for k in range(stage + 1, len(order)):
            for s in range(1, grid.size[order[k]]):
                copy = remote(
                    source,
                    here,
                    send.at[len(sends)],
                    recv.at[slot(place)],
                    grid.device(grid.moved(me, **{order[k]: s})),
                )
                copy.start()
                sends.append(copy)
    own.wait()
    for copy in sends:
        copy.wait_send()


def project_kernel(
    grid,
    window,
    chunk,
    x_ref,
    w_hbm,
    down_ref,
    up_ref,
    q_all,
    q_ref,
    nk_ref,
    nv_ref,
    w_ref,
    xs,
    xb,
    acc,
    p_ref,
    r_ref,
    t_ref,
    low_ref,
    q_own,
    w_sems,
    s1,
    r1,
    s2,
    r2,
    local,
    sems,
):
    me = grid.place()
    order = ("a", "b", "c")
    n = grid.wide
    at = grid.on_wide(me)
    rows = x_ref.shape[0]
    width = q_ref.shape[0]
    steps = 3 * width // chunk

    def load(i):
        part = pl.ds(i * chunk, chunk)
        return pltpu.make_async_copy(w_hbm.at[part], w_ref.at[part], w_sems.at[i])

    for i in range(steps):
        load(i).start()
    barrier = pltpu.get_barrier_semaphore()
    for d in range(1, n):
        pl.semaphore_signal(barrier, inc=1, device_id=(me["r"], (at + d) % n), device_id_type=MESH)
    pl.semaphore_wait(barrier, n - 1)
    spread(grid, me, order, x_ref, xs, s1, r1, local.at[0])

    def pack(i, carry):
        cols = pl.ds(pl.multiple_of(i * 1024, 1024), 1024)
        slabs = [xs[k, :, cols].astype(jnp.float32) for k in range(n)]
        xb[:, cols] = jnp.concatenate(slabs, axis=0).astype(jnp.bfloat16)
        return carry

    lax.fori_loop(0, D // 1024, pack, 0)
    xb[:, D:] = jnp.zeros((SPAN, xb.shape[1] - D), jnp.bfloat16)
    base = pl.multiple_of(at * width // 128 * 128, 128)
    partial = jnp.dot(xb[:, pl.ds(base, window)], down_ref[...], preferred_element_type=jnp.float32)
    for k in range(n):
        p_ref[k] = partial[k * rows : (k + 1) * rows]
    first = []
    for d in range(1, n):
        to = (at + d) % n
        copy = remote(p_ref.at[to], r_ref.at[d - 1], sems.at[0, d], sems.at[1, d], (me["r"], to))
        copy.start()
        first.append(copy)

    def multiply(i, carry):
        load(i).wait()
        part = pl.ds(pl.multiple_of(i * chunk, chunk), chunk)
        acc[part, :] = lax.dot_general(
            w_ref[part, :],
            xb[:, :D],
            (((1,), (1,)), ((), ())),
            preferred_element_type=jnp.float32,
        )
        return carry

    lax.fori_loop(0, steps // 2, multiply, 0)
    total = p_ref[at]
    for d, copy in enumerate(first):
        copy.wait_recv()
        total = total + r_ref[d]
    t_ref[...] = total.astype(t_ref.dtype)
    second = []
    for d in range(1, n):
        copy = remote(t_ref, low_ref.at[at], sems.at[2, d], sems.at[3, d], (me["r"], (at + d) % n))
        copy.start()
        second.append(copy)
    low_ref[at] = t_ref[...]
    lax.fori_loop(steps // 2, steps, multiply, 0)
    for d in range(1, n):
        source = (at + n - d) % n
        remote(
            t_ref, low_ref.at[source], sems.at[2, d], sems.at[3, d], (me["r"], at)
        ).wait_recv()
    lowrank = jnp.concatenate([low_ref[k].astype(jnp.float32) for k in range(n)], axis=0).astype(
        jnp.bfloat16
    )
    for c, out in enumerate((q_ref, nk_ref, nv_ref)):
        adapted = lax.dot_general(
            up_ref[c],
            lowrank[:, c * RANK : (c + 1) * RANK],
            (((1,), (1,)), ((), ())),
            preferred_element_type=jnp.float32,
        )
        value = (acc[c * width : (c + 1) * width, :] + adapted).astype(jnp.bfloat16)
        out[...] = value
        if c == 0:
            q_own[...] = value
    spread(grid, me, order, q_own, q_all, s2, r2, local.at[1])
    for copy in first + second:
        copy.wait_send()


def project(grid, normed, qkv_weight, adapter_down, adapter_up, collective_id):
    n = grid.wide
    rows = normed.shape[0]
    width = qkv_weight.shape[2]
    window = -(-(width + 128 - math.gcd(width, 128)) // 128) * 128
    shift = lax.axis_index("wide") * width % 128
    down = lax.dynamic_update_slice(
        jnp.zeros((window, 3 * RANK), jnp.bfloat16), adapter_down, (shift, 0)
    )
    weight = qkv_weight.transpose(1, 2, 0).reshape(3 * width, D)
    chunk = 224 if width % 224 == 0 else width
    vmem = pl.BlockSpec(memory_space=pltpu.VMEM)
    turned = jax.ShapeDtypeStruct((width, SPAN), jnp.bfloat16)
    dma = pltpu.SemaphoreType.DMA
    return pl.pallas_call(
        functools.partial(project_kernel, grid, window, chunk),
        out_shape=[jax.ShapeDtypeStruct((n, width, SPAN), jnp.bfloat16), turned, turned, turned],
        in_specs=[vmem, pl.BlockSpec(memory_space=pl.ANY), vmem, vmem],
        out_specs=[vmem] * 4,
        scratch_shapes=[
            pltpu.VMEM((3 * width, D), jnp.bfloat16),
            pltpu.VMEM((n, rows, D), jnp.bfloat16),
            pltpu.VMEM((SPAN, D + 256), jnp.bfloat16),
            pltpu.VMEM((3 * width, SPAN), jnp.float32),
            pltpu.VMEM((n, rows, 3 * RANK), jnp.float32),
            pltpu.VMEM((n - 1, rows, 3 * RANK), jnp.float32),
            pltpu.VMEM((rows, 3 * RANK), jnp.bfloat16),
            pltpu.VMEM((n, rows, 3 * RANK), jnp.bfloat16),
            pltpu.VMEM((width, SPAN), jnp.bfloat16),
            dma((3 * width // chunk,)),
            dma((n,)),
            dma((n,)),
            dma((n,)),
            dma((n,)),
            dma((2,)),
            dma((4, n)),
        ],
        compiler_params=params(collective_id),
        name="project",
    )(normed, weight, down, adapter_up.transpose(0, 2, 1))


def add_join(first, second):
    return [x + y for x, y in zip(first, second)]


def softmax_join(first, second):
    num1, st1 = first
    num2, st2 = second
    max1, sum1 = st1[..., :GROUP, :], st1[..., GROUP:, :]
    max2, sum2 = st2[..., :GROUP, :], st2[..., GROUP:, :]
    highest = jnp.maximum(max1, max2)
    f1 = jnp.exp(max1 - highest)
    f2 = jnp.exp(max2 - highest)
    heads = num1.shape[-3]
    num = jnp.stack(
        [
            num1[..., i, :, :] * f1[..., i : i + 1, :] + num2[..., i, :, :] * f2[..., i : i + 1, :]
            for i in range(heads)
        ],
        axis=-3,
    )
    return [num, jnp.concatenate([highest, sum1 * f1 + sum2 * f2], axis=-2)]


def combine_down(grid, me, reqs, join, ps, sc, sems):
    R, A, B = reqs, grid.size["a"], grid.size["b"]
    r, a, b, c = (me["r"] if R > 1 else 0), me["a"], me["b"], me["c"]
    parts = range(len(ps))
    sends = []
    count = [0]

    def push(pairs, device):
        out = []
        for i, (src, dst) in enumerate(pairs):
            k = count[0]
            count[0] += 1
            copy = remote(src, dst, sems.at[0, k], sems.at[1, k], device)
            copy.start()
            out.append(copy)
        sends.extend(out)
        return out

    def arrived(copies):
        for copy in copies:
            copy.wait_recv()

    def wide_values(refs):
        return [ref[...].astype(jnp.float32) for ref in refs]

    others = list(range(1, B)) + [0]
    core = {}
    peer = grid.device(grid.moved(me, c=1))
    for dr in list(range(1, R)) + [0]:
        rr = (r + dr) % R if dr else r
        for db in others:
            bb = (b + db) % B if db else b
            core[dr, db] = push(
                [(ps[i].at[rr, :, bb, 1 - c], sc["r1"][i].at[rr, bb]) for i in parts], peer
            )
    along_r = {}
    for dr in range(1, R):
        rr = (r + dr) % R
        for db in others:
            bb = (b + db) % B if db else b
            arrived(core[dr, db])
            both = join(
                wide_values([ps[i].at[rr, :, bb, c] for i in parts]),
                wide_values([sc["r1"][i].at[rr, bb] for i in parts]),
            )
            for i in parts:
                sc["t1"][i][rr, bb] = both[i].astype(sc["t1"][i].dtype)
            along_r[dr, db] = push(
                [(sc["t1"][i].at[rr, bb], sc["r2"][i].at[dr - 1, bb]) for i in parts],
                grid.device(grid.moved(me, r=dr)),
            )
    along_b = {}
    for db in others:
        bb = (b + db) % B if db else b
        arrived(core[0, db])
        both = join(
            wide_values([ps[i].at[r, :, bb, c] for i in parts]),
            wide_values([sc["r1"][i].at[r, bb] for i in parts]),
        )
        for dr in range(1, R):
            arrived(along_r[dr, db])
            both = join(both, wide_values([sc["r2"][i].at[dr - 1, bb] for i in parts]))
        if db:
            for i in parts:
                sc["t2"][i][bb] = both[i].astype(sc["t2"][i].dtype)
            along_b[db] = push(
                [(sc["t2"][i].at[bb], sc["r3"][i].at[db - 1]) for i in parts],
                grid.device(grid.moved(me, b=db)),
            )
    for db in range(1, B):
        arrived(along_b[db])
        both = join(both, wide_values([sc["r3"][i].at[db - 1] for i in parts]))
    for i in parts:
        sc["own"][i][...] = both[i]
        sc["t3"][i][...] = both[i].astype(sc["t3"][i].dtype)
    along_a = []
    for da in range(1, A):
        aa = (a + da) % A
        along_a.append(
            push(
                [(sc["t3"][i].at[aa], sc["r4"][i].at[da - 1]) for i in parts],
                grid.device(grid.moved(me, a=da)),
            )
        )
    total = [sc["own"][i][a] for i in parts]
    for da in range(1, A):
        arrived(along_a[da - 1])
        total = join(total, wide_values([sc["r4"][i].at[da - 1] for i in parts]))
    return total, sends


SCRATCH = ("r1", "t1", "r2", "t2", "r3", "own", "t3", "r4")


def reduce_scratch(grid, reqs, slabs):
    R, A, B = reqs, grid.size["a"], grid.size["b"]
    lead = dict(
        r1=(R, B, A),
        t1=(R if R > 1 else 1, B if R > 1 else 1, A if R > 1 else 1),
        r2=(R - 1, B, A) if R > 1 else (1, 1, 1),
        t2=(B, A),
        r3=(max(B - 1, 1), A),
        own=(A,),
        t3=(A,),
        r4=(max(A - 1, 1),),
    )
    shapes = []
    for name in SCRATCH:
        for shape, dtype in slabs:
            shapes.append(
                pltpu.VMEM(lead[name] + tuple(shape), jnp.float32 if name == "own" else dtype)
            )
    copies = (R * B + (R - 1) * B + (B - 1) + (A - 1)) * len(slabs)
    shapes.append(pltpu.SemaphoreType.DMA((2, copies)))
    return shapes


def reduce_kernel(grid, reqs, join, parts, *refs):
    ps, outs, rest, sems = refs[:parts], refs[parts : 2 * parts], refs[2 * parts : -1], refs[-1]
    sc = {name: rest[k * parts : (k + 1) * parts] for k, name in enumerate(SCRATCH)}
    me = grid.place()
    grid.barrier(me, ("r", "a", "b", "c") if reqs > 1 else ("a", "b", "c"))
    total, sends = combine_down(grid, me, reqs, join, ps, sc, sems)
    for out, value in zip(outs, total):
        out[...] = value.astype(out.dtype)
    for copy in sends:
        copy.wait_send()


def reduce_scatter(grid, reqs, join, arrays, out_dtypes, collective_id):
    A, B = grid.size["a"], grid.size["b"]
    slabs = [(x.shape[1:], x.dtype) for x in arrays]
    vmem = pl.BlockSpec(memory_space=pltpu.VMEM)
    return pl.pallas_call(
        functools.partial(reduce_kernel, grid, reqs, join, len(arrays)),
        out_shape=[jax.ShapeDtypeStruct(s, t) for (s, _), t in zip(slabs, out_dtypes)],
        in_specs=[vmem] * len(arrays),
        out_specs=[vmem] * len(arrays),
        scratch_shapes=reduce_scratch(grid, reqs, slabs),
        compiler_params=params(collective_id),
        name="reduce" + str(collective_id),
    )(*[x.reshape((reqs, A, B, 2) + x.shape[1:]) for x in arrays])


def middle_kernel(grid, p_ref, gain_ref, o_ref, mid_ref, *rest):
    scratch, sems, send, recv, local = rest[:-4], rest[-4], rest[-3], rest[-2], rest[-1]
    sc = {name: [scratch[k]] for k, name in enumerate(SCRATCH)}
    me = grid.place()
    grid.barrier(me, ("r", "a", "b", "c"))
    (total,), sends = combine_down(grid, me, 1, add_join, [p_ref], sc, sems)
    meansq = jnp.mean(total * total, axis=-1, keepdims=True)
    scaled = total * lax.rsqrt(meansq + EPSILON) * gain_ref[...].astype(jnp.float32)
    mid_ref[...] = scaled.astype(mid_ref.dtype)
    spread(grid, me, ("a", "b", "r", "c"), mid_ref, o_ref, send, recv, local)
    for copy in sends:
        copy.wait_send()


def middle(grid, part, gain, collective_id):
    slots = grid.size["r"] * grid.wide
    slab = part.shape[1:]
    vmem = pl.BlockSpec(memory_space=pltpu.VMEM)
    return pl.pallas_call(
        functools.partial(middle_kernel, grid),
        out_shape=jax.ShapeDtypeStruct((slots,) + slab, jnp.bfloat16),
        in_specs=[vmem, vmem],
        out_specs=vmem,
        scratch_shapes=[pltpu.VMEM(slab, jnp.bfloat16)]
        + reduce_scratch(grid, 1, [(slab, jnp.bfloat16)])
        + [
            pltpu.SemaphoreType.DMA((slots,)),
            pltpu.SemaphoreType.DMA((slots,)),
            pltpu.SemaphoreType.DMA,
        ],
        compiler_params=params(collective_id),
        name="middle",
    )(part.reshape((1, grid.size["a"], grid.size["b"], 2) + slab), gain.reshape(1, -1))


def cache_kernel(heads, q_ref, k_ref, v_ref, ok_ref, num_ref, st_ref):
    ok = ok_ref[...] > 0.0
    st_ref[...] = jnp.zeros_like(st_ref)
    for i in range(GROUP):
        keys = k_ref[0, :, i * HD : (i + 1) * HD]
        values = v_ref[0, :, i * HD : (i + 1) * HD]
        scores = jnp.dot(keys, q_ref[i], preferred_element_type=jnp.float32) * HD ** (-0.5)
        scores = jnp.where(ok, scores, NEG_LARGE)
        highest = jnp.max(scores, axis=0, keepdims=True)
        weights = jnp.where(ok, jnp.exp(scores - highest), 0.0)
        num = lax.dot_general(
            values,
            weights.astype(jnp.bfloat16),
            (((0,), (0,)), ((), ())),
            preferred_element_type=jnp.float32,
        )
        num_ref[i] = num.astype(jnp.bfloat16)
        slab, row = i // heads, i % heads
        st_ref[slab, row : row + 1, :] = highest
        st_ref[slab, GROUP + row : GROUP + row + 1, :] = jnp.sum(weights, axis=0, keepdims=True)


def cache_attention(heads, query, keys, values, usable):
    block = keys.shape[1]
    cols = GROUP * HD
    kv = pl.BlockSpec((1, block, cols), lambda i: (0, 0, i))
    return pl.pallas_call(
        functools.partial(cache_kernel, heads),
        grid=(HEADS // GROUP,),
        in_specs=[
            pl.BlockSpec((GROUP, HD, SPAN), lambda i: (i, 0, 0)),
            kv,
            kv,
            pl.BlockSpec((block, SPAN), lambda i: (0, 0)),
        ],
        out_specs=[
            pl.BlockSpec((GROUP, HD, SPAN), lambda i: (i, 0, 0)),
            pl.BlockSpec((GROUP // heads, 2 * GROUP, SPAN), lambda i: (i, 0, 0)),
        ],
        out_shape=[
            jax.ShapeDtypeStruct((HEADS, HD, SPAN), jnp.bfloat16),
            jax.ShapeDtypeStruct((HEADS // heads, 2 * GROUP, SPAN), jnp.float32),
        ],
        compiler_params=params(),
        name="cache_attention",
    )(query, keys, values, usable)


def body(
    grid,
    tokens,
    attn_gain,
    qkv_weight,
    adapter_down,
    adapter_up,
    out_weight,
    mlp_gain,
    gate_up,
    down_weight,
    key_cache,
    value_cache,
    cache_lengths,
    slot_mask,
    span_counts,
):
    reqs, wide = grid.size["r"], grid.wide
    rows = tokens.shape[0]
    width = qkv_weight.shape[2]
    heads = width // HD
    wide_index = lax.axis_index("wide")
    normed = rms_scale(tokens, attn_gain)
    query_all, query_turned, keys_turned, values_turned = project(
        grid, normed, qkv_weight, adapter_down, adapter_up, 0
    )
    new_keys = keys_turned.T
    new_values = values_turned.T
    query_all = query_all.reshape(HEADS, HD, SPAN)
    query_turned = query_turned.reshape(heads, HD, SPAN)

    block_len = key_cache.shape[1]
    positions = wide_index * block_len + jnp.arange(block_len)
    usable = ((positions < cache_lengths[0]) & (slot_mask[0] == 1)).astype(jnp.float32)
    usable = jnp.broadcast_to(usable[:, None], (block_len, SPAN))
    num, stats = cache_attention(heads, query_all, key_cache, value_cache, usable)
    cache_num, cache_stats = reduce_scatter(
        grid,
        1,
        softmax_join,
        [num.reshape(wide, heads, HD, SPAN), stats],
        [jnp.float32, jnp.float32],
        3,
    )

    span_count = span_counts[0]
    query_pos = jnp.arange(SPAN)[None, :]
    key_pos = jnp.arange(SPAN)[:, None]
    span_ok = (key_pos <= query_pos) & ((key_pos < span_count) | (key_pos == query_pos))
    own_scores = (
        jnp.einsum(
            "hdq,khd->hkq",
            query_turned,
            new_keys.reshape(SPAN, heads, HD),
            preferred_element_type=jnp.float32,
        )
        * HD ** (-0.5)
    )
    own_scores = jnp.where(span_ok, own_scores, NEG_LARGE)
    own_max = jnp.max(own_scores, axis=1)
    own_weights = jnp.where(span_ok, jnp.exp(own_scores - own_max[:, None]), 0.0)
    own_sum = jnp.sum(own_weights, axis=1)
    own_num = jnp.einsum(
        "hkq,khd->hdq",
        own_weights.astype(jnp.bfloat16),
        new_values.reshape(SPAN, heads, HD),
        preferred_element_type=jnp.float32,
    )
    cache_max, cache_sum = cache_stats[:heads], cache_stats[GROUP : GROUP + heads]
    highest = jnp.maximum(cache_max, own_max)
    cache_factor = jnp.exp(cache_max - highest)
    own_factor = jnp.exp(own_max - highest)
    totals = cache_sum * cache_factor + own_sum * own_factor
    mixed = cache_num * cache_factor[:, None] + own_num * own_factor[:, None]
    attention = (mixed / totals[:, None]).astype(jnp.bfloat16).reshape(width, SPAN).T

    attn_part = jnp.dot(attention, out_weight, preferred_element_type=jnp.float32)
    every_row = middle(
        grid, attn_part.astype(jnp.bfloat16).reshape(wide, rows, -1), mlp_gain, 4
    ).reshape(reqs * SPAN, -1)
    both = jnp.einsum("td,cfd->ctf", every_row, gate_up, preferred_element_type=jnp.float32)
    hidden = (jax.nn.silu(both[0]) * both[1]).astype(jnp.bfloat16)
    mlp_part = jnp.dot(hidden, down_weight, preferred_element_type=jnp.float32)
    (hidden_out,) = reduce_scatter(
        grid,
        reqs,
        add_join,
        [mlp_part.astype(jnp.bfloat16).reshape(reqs * wide, rows, -1)],
        [jnp.bfloat16],
        6,
    )
    return (hidden_out, attention, new_keys, new_values)


def solution(mesh):
    grid = Grid(mesh.shape["req"], mesh.shape["wide"])
    return jax.shard_map(
        functools.partial(body, grid),
        mesh=mesh,
        in_specs=(
            P(("req", "wide"), None),
            P(),
            P(None, None, "wide"),
            P("wide", None),
            P(None, None, "wide"),
            P("wide", None),
            P(),
            P(None, ("req", "wide"), None),
            P(("req", "wide"), None),
            P("req", "wide", None),
            P("req", "wide", None),
            P("req"),
            P("req", "wide"),
            P("req"),
        ),
        out_specs=(P(("req", "wide"), None), P("req", "wide"), P("req", "wide"), P("req", "wide")),
        check_vma=False,
    )
```

```python
import functools
import math

import jax
import jax.numpy as jnp
from jax import lax
from jax.experimental import pallas as pl
from jax.experimental.pallas import tpu as pltpu
from jax.sharding import PartitionSpec as P

D = 7168
HEADS = 32
HD = 224
RANK = 128
SPAN = 128
GROUP = 4

EPSILON = 1e-05
NEG_LARGE = -1e30
MESH = pl.DeviceIdType.MESH
VMEM_LIMIT = 48 * 1024 * 1024


def rms_scale(values, gains):
    widened = values.astype(jnp.float32)
    meansq = jnp.mean(widened * widened, axis=-1, keepdims=True)
    return (widened * lax.rsqrt(meansq + EPSILON) * gains.astype(jnp.float32)).astype(jnp.bfloat16)


def params(collective_id=None):
    if collective_id is None:
        return pltpu.CompilerParams(vmem_limit_bytes=VMEM_LIMIT)
    return pltpu.CompilerParams(
        collective_id=collective_id, has_side_effects=True, vmem_limit_bytes=VMEM_LIMIT
    )


class Grid:
    def __init__(self, reqs, wide):
        self.wide = wide
        chips = wide // 2
        first = 4 if chips % 4 == 0 else 1
        self.size = dict(r=reqs, a=first, b=chips // first, c=2)

    def place(self):
        me = lax.axis_index("wide")
        b = self.size["b"]
        return dict(
            r=lax.axis_index("req"), a=me // (2 * b), b=(me // 2) % b, c=me % 2
        )

    def moved(self, place, **steps):
        out = dict(place)
        for axis, step in steps.items():
            if step:
                out[axis] = (place[axis] + step) % self.size[axis]
        return out

    def on_wide(self, place):
        return (place["a"] * self.size["b"] + place["b"]) * 2 + place["c"]

    def device(self, place):
        return (place["r"], self.on_wide(place))

    def barrier(self, me, axes):
        sem = pltpu.get_barrier_semaphore()
        count = 0
        for axis in axes:
            for step in range(1, self.size[axis]):
                pl.semaphore_signal(
                    sem,
                    inc=1,
                    device_id=self.device(self.moved(me, **{axis: step})),
                    device_id_type=MESH,
                )
                count += 1
        pl.semaphore_wait(sem, count)


def remote(src, dst, send, recv, device):
    return pltpu.make_async_remote_copy(
        src_ref=src, dst_ref=dst, send_sem=send, recv_sem=recv, device_id=device, device_id_type=MESH
    )


def spread(grid, me, order, x_ref, o_ref, send, recv, local):
    def slot(place):
        at = grid.on_wide(place)
        return place["r"] * grid.wide + at if "r" in order else at

    own = pltpu.make_async_copy(x_ref, o_ref.at[slot(me)], local)
    own.start()
    items = [((0,) * len(order), -1)]
    for k, axis in enumerate(order):
        items += [
            (steps[:k] + (s,) + steps[k + 1 :], k)
            for steps, _ in list(items)
            for s in range(1, grid.size[axis])
        ]
    items.sort(key=lambda item: (sum(1 for s in item[0] if s), item[1]))
    sends = []
    for steps, stage in items:
        place = grid.moved(me, **dict(zip(order, steps)))
        here = o_ref.at[slot(place)]
        if stage >= 0:
            remote(x_ref, here, send.at[0], recv.at[slot(place)], grid.device(me)).wait_recv()
        source = here if stage >= 0 else x_ref
        for k in range(stage + 1, len(order)):
            for s in range(1, grid.size[order[k]]):
                copy = remote(
                    source,
                    here,
                    send.at[len(sends)],
                    recv.at[slot(place)],
                    grid.device(grid.moved(me, **{order[k]: s})),
                )
                copy.start()
                sends.append(copy)
    own.wait()
    for copy in sends:
        copy.wait_send()


def project_kernel(
    grid,
    window,
    chunk,
    x_ref,
    w_hbm,
    down_ref,
    up_ref,
    q_all,
    q_ref,
    nk_ref,
    nv_ref,
    w_ref,
    xs,
    xb,
    acc,
    p_ref,
    r_ref,
    t_ref,
    low_ref,
    q_own,
    w_sems,
    s1,
    r1,
    s2,
    r2,
    local,
    sems,
):
    me = grid.place()
    order = ("a", "b", "c")
    n = grid.wide
    at = grid.on_wide(me)
    rows = x_ref.shape[0]
    width = q_ref.shape[0]
    steps = 3 * width // chunk

    def load(i):
        part = pl.ds(i * chunk, chunk)
        return pltpu.make_async_copy(w_hbm.at[part], w_ref.at[part], w_sems.at[i])

    for i in range(steps):
        load(i).start()
    barrier = pltpu.get_barrier_semaphore()
    for d in range(1, n):
        pl.semaphore_signal(barrier, inc=1, device_id=(me["r"], (at + d) % n), device_id_type=MESH)
    pl.semaphore_wait(barrier, n - 1)
    spread(grid, me, order, x_ref, xs, s1, r1, local.at[0])

    def pack(i, carry):
        cols = pl.ds(pl.multiple_of(i * 1024, 1024), 1024)
        slabs = [xs[k, :, cols].astype(jnp.float32) for k in range(n)]
        xb[:, cols] = jnp.concatenate(slabs, axis=0).astype(jnp.bfloat16)
        return carry

    lax.fori_loop(0, D // 1024, pack, 0)
    xb[:, D:] = jnp.zeros((SPAN, xb.shape[1] - D), jnp.bfloat16)
    base = pl.multiple_of(at * width // 128 * 128, 128)
    partial = jnp.dot(xb[:, pl.ds(base, window)], down_ref[...], preferred_element_type=jnp.float32)
    for k in range(n):
        p_ref[k] = partial[k * rows : (k + 1) * rows]
    first = []
    for d in range(1, n):
        to = (at + d) % n
        copy = remote(p_ref.at[to], r_ref.at[d - 1], sems.at[0, d], sems.at[1, d], (me["r"], to))
        copy.start()
        first.append(copy)

    def multiply(i, carry):
        load(i).wait()
        part = pl.ds(pl.multiple_of(i * chunk, chunk), chunk)
        acc[part, :] = lax.dot_general(
            w_ref[part, :],
            xb[:, :D],
            (((1,), (1,)), ((), ())),
            preferred_element_type=jnp.float32,
        )
        return carry

    lax.fori_loop(0, steps // 2, multiply, 0)
    total = p_ref[at]
    for d, copy in enumerate(first):
        copy.wait_recv()
        total = total + r_ref[d]
    t_ref[...] = total.astype(t_ref.dtype)
    second = []
    for d in range(1, n):
        copy = remote(t_ref, low_ref.at[at], sems.at[2, d], sems.at[3, d], (me["r"], (at + d) % n))
        copy.start()
        second.append(copy)
    low_ref[at] = t_ref[...]
    lax.fori_loop(steps // 2, steps, multiply, 0)
    for d in range(1, n):
        source = (at + n - d) % n
        remote(
            t_ref, low_ref.at[source], sems.at[2, d], sems.at[3, d], (me["r"], at)
        ).wait_recv()
    lowrank = jnp.concatenate([low_ref[k].astype(jnp.float32) for k in range(n)], axis=0).astype(
        jnp.bfloat16
    )
    for c, out in enumerate((q_ref, nk_ref, nv_ref)):
        adapted = lax.dot_general(
            up_ref[c],
            lowrank[:, c * RANK : (c + 1) * RANK],
            (((1,), (1,)), ((), ())),
            preferred_element_type=jnp.float32,
        )
        value = (acc[c * width : (c + 1) * width, :] + adapted).astype(jnp.bfloat16)
        out[...] = value
        if c == 0:
            q_own[...] = value
    spread(grid, me, order, q_own, q_all, s2, r2, local.at[1])
    for copy in first + second:
        copy.wait_send()


def project(grid, normed, qkv_weight, adapter_down, adapter_up, collective_id):
    n = grid.wide
    rows = normed.shape[0]
    width = qkv_weight.shape[2]
    window = -(-(width + 128 - math.gcd(width, 128)) // 128) * 128
    shift = lax.axis_index("wide") * width % 128
    down = lax.dynamic_update_slice(
        jnp.zeros((window, 3 * RANK), jnp.bfloat16), adapter_down, (shift, 0)
    )
    weight = qkv_weight.transpose(1, 2, 0).reshape(3 * width, D)
    chunk = 224 if width % 224 == 0 else width
    vmem = pl.BlockSpec(memory_space=pltpu.VMEM)
    turned = jax.ShapeDtypeStruct((width, SPAN), jnp.bfloat16)
    dma = pltpu.SemaphoreType.DMA
    return pl.pallas_call(
        functools.partial(project_kernel, grid, window, chunk),
        out_shape=[jax.ShapeDtypeStruct((n, width, SPAN), jnp.bfloat16), turned, turned, turned],
        in_specs=[vmem, pl.BlockSpec(memory_space=pl.ANY), vmem, vmem],
        out_specs=[vmem] * 4,
        scratch_shapes=[
            pltpu.VMEM((3 * width, D), jnp.bfloat16),
            pltpu.VMEM((n, rows, D), jnp.bfloat16),
            pltpu.VMEM((SPAN, D + 256), jnp.bfloat16),
            pltpu.VMEM((3 * width, SPAN), jnp.float32),
            pltpu.VMEM((n, rows, 3 * RANK), jnp.float32),
            pltpu.VMEM((n - 1, rows, 3 * RANK), jnp.float32),
            pltpu.VMEM((rows, 3 * RANK), jnp.bfloat16),
            pltpu.VMEM((n, rows, 3 * RANK), jnp.bfloat16),
            pltpu.VMEM((width, SPAN), jnp.bfloat16),
            dma((3 * width // chunk,)),
            dma((n,)),
            dma((n,)),
            dma((n,)),
            dma((n,)),
            dma((2,)),
            dma((4, n)),
        ],
        compiler_params=params(collective_id),
        name="project",
    )(normed, weight, down, adapter_up.transpose(0, 2, 1))


def add_join(first, second):
    return [x + y for x, y in zip(first, second)]


def softmax_join(first, second):
    num1, st1 = first
    num2, st2 = second
    max1, sum1 = st1[..., :GROUP, :], st1[..., GROUP:, :]
    max2, sum2 = st2[..., :GROUP, :], st2[..., GROUP:, :]
    highest = jnp.maximum(max1, max2)
    f1 = jnp.exp(max1 - highest)
    f2 = jnp.exp(max2 - highest)
    heads = num1.shape[-3]
    num = jnp.stack(
        [
            num1[..., i, :, :] * f1[..., i : i + 1, :] + num2[..., i, :, :] * f2[..., i : i + 1, :]
            for i in range(heads)
        ],
        axis=-3,
    )
    return [num, jnp.concatenate([highest, sum1 * f1 + sum2 * f2], axis=-2)]


def loop(count, step):
    if count == 1:
        step(0)
    else:
        lax.fori_loop(0, count, lambda i, carry: (step(i), carry)[1], 0)


def combine_down(grid, me, reqs, join, ps, sc, sems, produce=None):
    R, A, B = reqs, grid.size["a"], grid.size["b"]
    r, a, b, c = (me["r"] if R > 1 else 0), me["a"], me["b"], me["c"]
    n = len(ps)
    parts = range(n)
    base_r = R * B * A * n
    base_b = base_r + (R - 1) * B * A * n
    base_a = base_b + (B - 1) * A * n
    db_order = list(range(1, B)) + [0]
    dr_order = list(range(1, R)) + [0]

    def where(dr, db, i):
        rr = (r + dr) % R if dr else r
        bb = (b + db) % B if db else b
        return rr, (a + i + 1) % A, bb

    def copies(base, pairs, device):
        return [
            remote(src, dst, sems.at[0, base + k], sems.at[1, base + k], device)
            for k, (src, dst) in enumerate(pairs)
        ]

    def core(dr, db, i):
        rr, aa, bb = where(dr, db, i)
        return copies(
            ((dr * B + db) * A + i) * n,
            [(ps[k].at[rr, aa, bb, 1 - c], sc["r1"][k].at[dr, db, i]) for k in parts],
            grid.device(grid.moved(me, c=1)),
        )

    def along_r(dr, db, i):
        return copies(
            base_r + (((dr - 1) * B + db) * A + i) * n,
            [(sc["t1"][k].at[dr - 1, db, i], sc["r2"][k].at[dr - 1, db, i]) for k in parts],
            grid.device(grid.moved(me, r=dr)),
        )

    def along_b(db, i):
        return copies(
            base_b + ((db - 1) * A + i) * n,
            [(sc["t2"][k].at[db - 1, i], sc["r3"][k].at[db - 1, i]) for k in parts],
            grid.device(grid.moved(me, b=db)),
        )

    def along_a(da):
        return copies(
            base_a + (da - 1) * n,
            [(sc["t3"][k].at[da - 1], sc["r4"][k].at[da - 1]) for k in parts],
            grid.device(dict(me, a=(a + da) % A)),
        )

    def start(made):
        for copy in made:
            copy.start()

    def arrived(made):
        for copy in made:
            copy.wait_recv()

    def wide_values(refs):
        return [ref[...].astype(jnp.float32) for ref in refs]

    def at_chip(dr, db, i):
        rr, aa, bb = where(dr, db, i)
        arrived(core(dr, db, i))
        both = join(
            wide_values([ps[k].at[rr, aa, bb, c] for k in parts]),
            wide_values([sc["r1"][k].at[dr, db, i] for k in parts]),
        )
        if dr == 0:
            for step in range(1, R):
                arrived(along_r(step, db, i))
                both = join(both, wide_values([sc["r2"][k].at[step - 1, db, i] for k in parts]))
        return both

    def keep(name, at, values):
        for k in parts:
            sc[name][k][at] = values[k].astype(sc[name][k].dtype)

    def to_r(dr, db, i):
        keep("t1", (dr - 1, db, i), at_chip(dr, db, i))
        start(along_r(dr, db, i))

    def to_b(db, i):
        keep("t2", (db - 1, i), at_chip(0, db, i))
        start(along_b(db, i))

    def on_b(i):
        both = at_chip(0, 0, i)
        for db in range(1, B):
            arrived(along_b(db, i))
            both = join(both, wide_values([sc["r3"][k].at[db - 1, i] for k in parts]))
        return both

    def to_a(i):
        keep("t3", (i,), on_b(i))
        start(along_a(i + 1))

    if produce is None:
        for dr in dr_order:
            for db in db_order:
                loop(A, lambda i: start(core(dr, db, i)))
        for dr in range(1, R):
            for db in db_order:
                loop(A, lambda i: to_r(dr, db, i))
        for db in range(1, B):
            loop(A, lambda i: to_b(db, i))
    else:
        before = None
        for db in db_order:

            def step(i):
                produce(where(0, db, i))
                start(core(0, db, i))
                if before:
                    pl.when(i == 0)(lambda: to_b(before, A - 1))
                if db:
                    pl.when(i > 0)(lambda: to_b(db, i - 1))

            lax.fori_loop(0, A, lambda i, carry: (step(i), carry)[1], 0)
            before = db
    if A > 1:
        loop(A - 1, to_a)
    total = on_b(A - 1)
    for da in range(1, A):
        arrived(along_a(da))
        total = join(total, wide_values([sc["r4"][k].at[da - 1] for k in parts]))

    def finish():
        def sent(made):
            for copy in made:
                copy.wait_send()

        for dr in range(R):
            for db in range(B):
                loop(A, lambda i: sent(core(dr, db, i)))
                if dr:
                    loop(A, lambda i: sent(along_r(dr, db, i)))
        for db in range(1, B):
            loop(A, lambda i: sent(along_b(db, i)))
        for da in range(1, A):
            sent(along_a(da))

    return total, finish


SCRATCH = ("r1", "t1", "r2", "t2", "r3", "t3", "r4")


def reduce_scratch(grid, reqs, slabs):
    R, A, B = reqs, grid.size["a"], grid.size["b"]
    lead = dict(
        r1=(R, B, A),
        t1=(R - 1, B, A) if R > 1 else (1, 1, 1),
        r2=(R - 1, B, A) if R > 1 else (1, 1, 1),
        t2=(max(B - 1, 1), A),
        r3=(max(B - 1, 1), A),
        t3=(max(A - 1, 1),),
        r4=(max(A - 1, 1),),
    )
    shapes = [
        pltpu.VMEM(lead[name] + tuple(shape), dtype) for name in SCRATCH for shape, dtype in slabs
    ]
    count = (R * B * A + (R - 1) * B * A + (B - 1) * A + (A - 1)) * len(slabs)
    shapes.append(pltpu.SemaphoreType.DMA((2, count)))
    return shapes


def reduce_kernel(grid, reqs, p_ref, o_ref, *rest):
    sems = rest[-1]
    sc = {name: [rest[k]] for k, name in enumerate(SCRATCH)}
    me = grid.place()
    grid.barrier(me, ("r", "a", "b", "c"))
    (total,), finish = combine_down(grid, me, reqs, add_join, [p_ref], sc, sems)
    o_ref[...] = total.astype(o_ref.dtype)
    finish()


def reduce_scatter(grid, reqs, x, out_dtype, collective_id):
    slab = x.shape[1:]
    vmem = pl.BlockSpec(memory_space=pltpu.VMEM)
    return pl.pallas_call(
        functools.partial(reduce_kernel, grid, reqs),
        out_shape=jax.ShapeDtypeStruct(slab, out_dtype),
        in_specs=[vmem],
        out_specs=vmem,
        scratch_shapes=reduce_scratch(grid, reqs, [(slab, x.dtype)]),
        compiler_params=params(collective_id),
        name="reduce" + str(collective_id),
    )(x.reshape((reqs, grid.size["a"], grid.size["b"], 2) + slab))


def cache_kernel(
    grid, heads, q_ref, k_hbm, v_hbm, ok_ref, num_out, st_out, k_ref, v_ref, num, st, loads, *rest
):
    sems = rest[-1]
    sc = {name: rest[2 * k : 2 * k + 2] for k, name in enumerate(SCRATCH)}
    me = grid.place()
    B = grid.size["b"]
    groups = HEADS // GROUP
    slabs = GROUP // heads

    def load(g):
        cols = pl.ds(pl.multiple_of(g * GROUP * HD, GROUP * HD), GROUP * HD)
        return [
            pltpu.make_async_copy(hbm.at[0, :, cols], ref.at[g], loads.at[k, g])
            for k, (hbm, ref) in enumerate(((k_hbm, k_ref), (v_hbm, v_ref)))
        ]

    def group(g):
        for copy in load(g):
            copy.wait()
        ok = ok_ref[...] > 0.0
        for j in range(slabs):
            slab = g * slabs + j
            at = (0, slab // (2 * B), (slab // 2) % B, slab % 2)
            tops, sums = [], []
            for h in range(heads):
                lanes = slice((j * heads + h) * HD, (j * heads + h + 1) * HD)
                scores = jnp.dot(
                    k_ref[g, :, lanes], q_ref[slab, h], preferred_element_type=jnp.float32
                ) * HD ** (-0.5)
                scores = jnp.where(ok, scores, NEG_LARGE)
                top = jnp.max(scores, axis=0, keepdims=True)
                weights = jnp.where(ok, jnp.exp(scores - top), 0.0)
                num[at + (h,)] = lax.dot_general(
                    v_ref[g, :, lanes],
                    weights.astype(jnp.bfloat16),
                    (((0,), (0,)), ((), ())),
                    preferred_element_type=jnp.float32,
                ).astype(jnp.bfloat16)
                tops.append(top)
                sums.append(jnp.sum(weights, axis=0, keepdims=True))
            blank = [jnp.zeros((GROUP - heads, SPAN), jnp.float32)]
            st[at] = jnp.concatenate(tops + blank + sums + blank, axis=0)

    loop(groups, lambda g: [copy.start() for copy in load(g)] and None)
    grid.barrier(me, ("a", "b", "c"))
    if slabs == 2:
        produce = lambda place: group(place[1] * B + place[2])
    else:
        loop(groups, group)
        produce = None
    total, finish = combine_down(grid, me, 1, softmax_join, [num, st], sc, sems, produce)
    num_out[...] = total[0]
    st_out[...] = total[1]
    finish()


def cache_attention(grid, heads, query, keys, values, usable, collective_id):
    block = keys.shape[1]
    groups = HEADS // GROUP
    lead = (1, grid.size["a"], grid.size["b"], 2)
    num = ((heads, HD, SPAN), jnp.bfloat16)
    stats = ((2 * GROUP, SPAN), jnp.float32)
    vmem = pl.BlockSpec(memory_space=pltpu.VMEM)
    hbm = pl.BlockSpec(memory_space=pl.ANY)
    return pl.pallas_call(
        functools.partial(cache_kernel, grid, heads),
        in_specs=[vmem, hbm, hbm, vmem],
        out_specs=[vmem, vmem],
        out_shape=[
            jax.ShapeDtypeStruct(num[0], jnp.float32),
            jax.ShapeDtypeStruct(stats[0], jnp.float32),
        ],
        scratch_shapes=[
            pltpu.VMEM((groups, block, GROUP * HD), jnp.bfloat16),
            pltpu.VMEM((groups, block, GROUP * HD), jnp.bfloat16),
            pltpu.VMEM(lead + num[0], num[1]),
            pltpu.VMEM(lead + stats[0], stats[1]),
            pltpu.SemaphoreType.DMA((2, groups)),
        ]
        + reduce_scratch(grid, 1, [num, stats]),
        compiler_params=params(collective_id),
        name="cache_attention",
    )(query, keys, values, usable)


def middle_kernel(grid, p_ref, gain_ref, o_ref, mid_ref, *rest):
    scratch, sems, send, recv, local = rest[:-4], rest[-4], rest[-3], rest[-2], rest[-1]
    sc = {name: [scratch[k]] for k, name in enumerate(SCRATCH)}
    me = grid.place()
    grid.barrier(me, ("r", "a", "b", "c"))
    (total,), finish = combine_down(grid, me, 1, add_join, [p_ref], sc, sems)
    meansq = jnp.mean(total * total, axis=-1, keepdims=True)
    scaled = total * lax.rsqrt(meansq + EPSILON) * gain_ref[...].astype(jnp.float32)
    mid_ref[...] = scaled.astype(mid_ref.dtype)
    spread(grid, me, ("a", "b", "r", "c"), mid_ref, o_ref, send, recv, local)
    finish()


def middle(grid, part, gain, collective_id):
    slots = grid.size["r"] * grid.wide
    slab = part.shape[1:]
    vmem = pl.BlockSpec(memory_space=pltpu.VMEM)
    return pl.pallas_call(
        functools.partial(middle_kernel, grid),
        out_shape=jax.ShapeDtypeStruct((slots,) + slab, jnp.bfloat16),
        in_specs=[vmem, vmem],
        out_specs=vmem,
        scratch_shapes=[pltpu.VMEM(slab, jnp.bfloat16)]
        + reduce_scratch(grid, 1, [(slab, jnp.bfloat16)])
        + [
            pltpu.SemaphoreType.DMA((slots,)),
            pltpu.SemaphoreType.DMA((slots,)),
            pltpu.SemaphoreType.DMA,
        ],
        compiler_params=params(collective_id),
        name="middle",
    )(part.reshape((1, grid.size["a"], grid.size["b"], 2) + slab), gain.reshape(1, -1))


def body(
    grid,
    tokens,
    attn_gain,
    qkv_weight,
    adapter_down,
    adapter_up,
    out_weight,
    mlp_gain,
    gate_up,
    down_weight,
    key_cache,
    value_cache,
    cache_lengths,
    slot_mask,
    span_counts,
):
    reqs, wide = grid.size["r"], grid.wide
    rows = tokens.shape[0]
    width = qkv_weight.shape[2]
    heads = width // HD
    wide_index = lax.axis_index("wide")
    normed = rms_scale(tokens, attn_gain)
    query_all, query_turned, keys_turned, values_turned = project(
        grid, normed, qkv_weight, adapter_down, adapter_up, 0
    )
    new_keys = keys_turned.T
    new_values = values_turned.T
    query_all = query_all.reshape(wide, heads, HD, SPAN)
    query_turned = query_turned.reshape(heads, HD, SPAN)

    block_len = key_cache.shape[1]
    positions = wide_index * block_len + jnp.arange(block_len)
    usable = ((positions < cache_lengths[0]) & (slot_mask[0] == 1)).astype(jnp.float32)
    usable = jnp.broadcast_to(usable[:, None], (block_len, SPAN))
    cache_num, cache_stats = cache_attention(
        grid, heads, query_all, key_cache, value_cache, usable, 3
    )

    span_count = span_counts[0]
    query_pos = jnp.arange(SPAN)[None, :]
    key_pos = jnp.arange(SPAN)[:, None]
    span_ok = (key_pos <= query_pos) & ((key_pos < span_count) | (key_pos == query_pos))
    own_scores = (
        jnp.einsum(
            "hdq,khd->hkq",
            query_turned,
            new_keys.reshape(SPAN, heads, HD),
            preferred_element_type=jnp.float32,
        )
        * HD ** (-0.5)
    )
    own_scores = jnp.where(span_ok, own_scores, NEG_LARGE)
    own_max = jnp.max(own_scores, axis=1)
    own_weights = jnp.where(span_ok, jnp.exp(own_scores - own_max[:, None]), 0.0)
    own_sum = jnp.sum(own_weights, axis=1)
    own_num = jnp.einsum(
        "hkq,khd->hdq",
        own_weights.astype(jnp.bfloat16),
        new_values.reshape(SPAN, heads, HD),
        preferred_element_type=jnp.float32,
    )
    cache_max, cache_sum = cache_stats[:heads], cache_stats[GROUP : GROUP + heads]
    highest = jnp.maximum(cache_max, own_max)
    cache_factor = jnp.exp(cache_max - highest)
    own_factor = jnp.exp(own_max - highest)
    totals = cache_sum * cache_factor + own_sum * own_factor
    mixed = cache_num * cache_factor[:, None] + own_num * own_factor[:, None]
    attention = (mixed / totals[:, None]).astype(jnp.bfloat16).reshape(width, SPAN).T

    attn_part = jnp.dot(attention, out_weight, preferred_element_type=jnp.float32)
    every_row = middle(
        grid, attn_part.astype(jnp.bfloat16).reshape(wide, rows, -1), mlp_gain, 4
    ).reshape(reqs * SPAN, -1)
    both = jnp.einsum("td,cfd->ctf", every_row, gate_up, preferred_element_type=jnp.float32)
    hidden = (jax.nn.silu(both[0]) * both[1]).astype(jnp.bfloat16)
    mlp_part = jnp.dot(hidden, down_weight, preferred_element_type=jnp.float32)
    hidden_out = reduce_scatter(
        grid,
        reqs,
        mlp_part.astype(jnp.bfloat16).reshape(reqs * wide, rows, -1),
        jnp.bfloat16,
        6,
    )
    return (hidden_out, attention, new_keys, new_values)


def solution(mesh):
    grid = Grid(mesh.shape["req"], mesh.shape["wide"])
    return jax.shard_map(
        functools.partial(body, grid),
        mesh=mesh,
        in_specs=(
            P(("req", "wide"), None),
            P(),
            P(None, None, "wide"),
            P("wide", None),
            P(None, None, "wide"),
            P("wide", None),
            P(),
            P(None, ("req", "wide"), None),
            P(("req", "wide"), None),
            P("req", "wide", None),
            P("req", "wide", None),
            P("req"),
            P("req", "wide"),
            P("req"),
        ),
        out_specs=(P(("req", "wide"), None), P("req", "wide"), P("req", "wide"), P("req", "wide")),
        check_vma=False,
    )
```

```python
import functools
import math

import jax
import jax.numpy as jnp
from jax import lax
from jax.experimental import pallas as pl
from jax.experimental.pallas import tpu as pltpu
from jax.sharding import PartitionSpec as P

D = 7168
HEADS = 32
HD = 224
RANK = 128
SPAN = 128
GROUP = 4

EPSILON = 1e-05
NEG_LARGE = -1e30
MESH = pl.DeviceIdType.MESH
VMEM_LIMIT = 48 * 1024 * 1024


def rms_scale(values, gains):
    widened = values.astype(jnp.float32)
    meansq = jnp.mean(widened * widened, axis=-1, keepdims=True)
    return (widened * lax.rsqrt(meansq + EPSILON) * gains.astype(jnp.float32)).astype(jnp.bfloat16)


def params(collective_id=None):
    if collective_id is None:
        return pltpu.CompilerParams(vmem_limit_bytes=VMEM_LIMIT)
    return pltpu.CompilerParams(
        collective_id=collective_id, has_side_effects=True, vmem_limit_bytes=VMEM_LIMIT
    )


class Grid:
    def __init__(self, reqs, wide):
        self.wide = wide
        chips = wide // 2
        first = 4 if chips % 4 == 0 else 1
        self.size = dict(r=reqs, a=first, b=chips // first, c=2)

    def place(self):
        me = lax.axis_index("wide")
        b = self.size["b"]
        return dict(
            r=lax.axis_index("req"), a=me // (2 * b), b=(me // 2) % b, c=me % 2
        )

    def moved(self, place, **steps):
        out = dict(place)
        for axis, step in steps.items():
            if step:
                out[axis] = (place[axis] + step) % self.size[axis]
        return out

    def on_wide(self, place):
        return (place["a"] * self.size["b"] + place["b"]) * 2 + place["c"]

    def device(self, place):
        return (place["r"], self.on_wide(place))

    def barrier(self, me, axes):
        sem = pltpu.get_barrier_semaphore()
        count = 0
        for axis in axes:
            for step in range(1, self.size[axis]):
                pl.semaphore_signal(
                    sem,
                    inc=1,
                    device_id=self.device(self.moved(me, **{axis: step})),
                    device_id_type=MESH,
                )
                count += 1
        pl.semaphore_wait(sem, count)


def remote(src, dst, send, recv, device):
    return pltpu.make_async_remote_copy(
        src_ref=src, dst_ref=dst, send_sem=send, recv_sem=recv, device_id=device, device_id_type=MESH
    )


def spread(grid, me, order, x_ref, o_ref, send, recv, local):
    a, A = me["a"], grid.size["a"]
    rest = order[1:]

    def slot(place):
        at = grid.on_wide(place)
        return place["r"] * grid.wide + at if "r" in order else at

    def guarded(cond, action):
        if cond is None:
            action()
        else:
            pl.when(cond)(action)

    own = pltpu.make_async_copy(x_ref, o_ref.at[slot(me)], local)
    own.start()
    hops = [((0,) * len(rest), -1)]
    for k, axis in enumerate(rest):
        hops += [
            (steps[:k] + (s,) + steps[k + 1 :], k)
            for steps, _ in list(hops)
            for s in range(1, grid.size[axis])
        ]
    lines = [(0, 0)] + [(d, sign) for d in range(1, A) for sign in (-1, 1)]
    items = [(d, sign, steps, stage) for d, sign in lines for steps, stage in hops]
    items.sort(key=lambda item: (item[0] + sum(1 for s in item[2] if s), item[3]))
    sends = []
    for d, sign, steps, stage in items:
        there = None if d == 0 else (a >= d if sign < 0 else a + d < A)
        place = dict(grid.moved(me, **dict(zip(rest, steps))))
        place["a"] = (a + sign * d + A) % A
        here = o_ref.at[slot(place)]
        is_own = d == 0 and stage < 0
        source = x_ref if is_own else here
        made = []

        def add(device, cond):
            copy = remote(source, here, send.at[len(sends)], recv.at[slot(place)], device)
            made.append((copy, cond))
            sends.append((copy, cond))

        if stage < 0:
            for way in (1, -1):
                if d == 0 or way == -sign:
                    room = a + 1 < A if way > 0 else a > 0
                    cond = room if there is None else jnp.logical_and(there, room)
                    add(grid.device(dict(me, a=(a + way + A) % A)), cond)
        for k in range(stage + 1, len(rest)):
            for s in range(1, grid.size[rest[k]]):
                add(grid.device(grid.moved(me, **{rest[k]: s})), there)
        if not is_own:
            landing = remote(x_ref, here, send.at[0], recv.at[slot(place)], grid.device(me))
            guarded(there, landing.wait_recv)
        for copy, cond in made:
            guarded(cond, copy.start)
    own.wait()
    for copy, cond in sends:
        guarded(cond, copy.wait_send)


def project_kernel(
    grid,
    window,
    chunk,
    tokens_ref,
    gain_ref,
    w_hbm,
    down_ref,
    up_ref,
    q_all,
    q_ref,
    nk_ref,
    nv_ref,
    w_ref,
    xs,
    xb,
    acc,
    p_ref,
    r_ref,
    t_ref,
    low_ref,
    q_own,
    x_ref,
    w_sems,
    s1,
    r1,
    s2,
    r2,
    local,
    sems,
):
    me = grid.place()
    order = ("a", "b", "c")
    n = grid.wide
    at = grid.on_wide(me)
    rows = tokens_ref.shape[0]
    width = q_ref.shape[0]
    steps = 3 * width // chunk

    def load(i):
        part = pl.ds(i * chunk, chunk)
        return pltpu.make_async_copy(w_hbm.at[part], w_ref.at[part], w_sems.at[i])

    barrier = pltpu.get_barrier_semaphore()
    for d in range(1, n):
        pl.semaphore_signal(barrier, inc=1, device_id=(me["r"], (at + d) % n), device_id_type=MESH)
    for i in range(steps):
        load(i).start()
    x_ref[...] = rms_scale(tokens_ref[...], gain_ref[...])
    pl.semaphore_wait(barrier, n - 1)
    spread(grid, me, order, x_ref, xs, s1, r1, local.at[0])

    def pack(i, carry):
        cols = pl.ds(pl.multiple_of(i * 1024, 1024), 1024)
        slabs = [xs[k, :, cols].astype(jnp.float32) for k in range(n)]
        xb[:, cols] = jnp.concatenate(slabs, axis=0).astype(jnp.bfloat16)
        return carry

    lax.fori_loop(0, D // 1024, pack, 0)
    xb[:, D:] = jnp.zeros((SPAN, xb.shape[1] - D), jnp.bfloat16)
    base = pl.multiple_of(at * width // 128 * 128, 128)
    partial = jnp.dot(xb[:, pl.ds(base, window)], down_ref[...], preferred_element_type=jnp.float32)
    for k in range(n):
        p_ref[k] = partial[k * rows : (k + 1) * rows]
    first = []
    for d in range(1, n):
        to = (at + d) % n
        copy = remote(p_ref.at[to], r_ref.at[d - 1], sems.at[0, d], sems.at[1, d], (me["r"], to))
        copy.start()
        first.append(copy)

    def multiply(i, carry):
        load(i).wait()
        part = pl.ds(pl.multiple_of(i * chunk, chunk), chunk)
        acc[part, :] = lax.dot_general(
            w_ref[part, :],
            xb[:, :D],
            (((1,), (1,)), ((), ())),
            preferred_element_type=jnp.float32,
        )
        return carry

    lax.fori_loop(0, steps // 2, multiply, 0)
    total = p_ref[at]
    for d, copy in enumerate(first):
        copy.wait_recv()
        total = total + r_ref[d]
    t_ref[...] = total.astype(t_ref.dtype)
    second = []
    for d in range(1, n):
        copy = remote(t_ref, low_ref.at[at], sems.at[2, d], sems.at[3, d], (me["r"], (at + d) % n))
        copy.start()
        second.append(copy)
    low_ref[at] = t_ref[...]
    lax.fori_loop(steps // 2, steps, multiply, 0)
    for d in range(1, n):
        source = (at + n - d) % n
        remote(
            t_ref, low_ref.at[source], sems.at[2, d], sems.at[3, d], (me["r"], at)
        ).wait_recv()
    lowrank = jnp.concatenate([low_ref[k].astype(jnp.float32) for k in range(n)], axis=0).astype(
        jnp.bfloat16
    )
    for c, out in enumerate((q_ref, nk_ref, nv_ref)):
        adapted = lax.dot_general(
            up_ref[c],
            lowrank[:, c * RANK : (c + 1) * RANK],
            (((1,), (1,)), ((), ())),
            preferred_element_type=jnp.float32,
        )
        value = (acc[c * width : (c + 1) * width, :] + adapted).astype(jnp.bfloat16)
        out[...] = value
        if c == 0:
            q_own[...] = value
    spread(grid, me, order, q_own, q_all, s2, r2, local.at[1])
    for copy in first + second:
        copy.wait_send()


def project(grid, tokens, gain, qkv_weight, adapter_down, adapter_up, collective_id):
    n = grid.wide
    rows = tokens.shape[0]
    width = qkv_weight.shape[2]
    window = -(-(width + 128 - math.gcd(width, 128)) // 128) * 128
    shift = lax.axis_index("wide") * width % 128
    down = lax.dynamic_update_slice(
        jnp.zeros((window, 3 * RANK), jnp.bfloat16), adapter_down, (shift, 0)
    )
    weight = qkv_weight.transpose(1, 2, 0).reshape(3 * width, D)
    chunk = 224 if width % 224 == 0 else width
    vmem = pl.BlockSpec(memory_space=pltpu.VMEM)
    turned = jax.ShapeDtypeStruct((width, SPAN), jnp.bfloat16)
    dma = pltpu.SemaphoreType.DMA
    return pl.pallas_call(
        functools.partial(project_kernel, grid, window, chunk),
        out_shape=[jax.ShapeDtypeStruct((n, width, SPAN), jnp.bfloat16), turned, turned, turned],
        in_specs=[vmem, vmem, pl.BlockSpec(memory_space=pl.ANY), vmem, vmem],
        out_specs=[vmem] * 4,
        scratch_shapes=[
            pltpu.VMEM((3 * width, D), jnp.bfloat16),
            pltpu.VMEM((n, rows, D), jnp.bfloat16),
            pltpu.VMEM((SPAN, D + 256), jnp.bfloat16),
            pltpu.VMEM((3 * width, SPAN), jnp.float32),
            pltpu.VMEM((n, rows, 3 * RANK), jnp.float32),
            pltpu.VMEM((n - 1, rows, 3 * RANK), jnp.float32),
            pltpu.VMEM((rows, 3 * RANK), jnp.bfloat16),
            pltpu.VMEM((n, rows, 3 * RANK), jnp.bfloat16),
            pltpu.VMEM((width, SPAN), jnp.bfloat16),
            pltpu.VMEM((rows, D), jnp.bfloat16),
            dma((3 * width // chunk,)),
            dma((2 * n + 2,)),
            dma((n,)),
            dma((2 * n + 2,)),
            dma((n,)),
            dma((2,)),
            dma((4, n)),
        ],
        compiler_params=params(collective_id),
        name="project",
    )(tokens, gain.reshape(1, -1), weight, down, adapter_up.transpose(0, 2, 1))


def add_join(first, second):
    return [x + y for x, y in zip(first, second)]


def softmax_join(first, second):
    num1, st1 = first
    num2, st2 = second
    max1, sum1 = st1[..., :GROUP, :], st1[..., GROUP:, :]
    max2, sum2 = st2[..., :GROUP, :], st2[..., GROUP:, :]
    highest = jnp.maximum(max1, max2)
    f1 = jnp.exp(max1 - highest)
    f2 = jnp.exp(max2 - highest)
    heads = num1.shape[-3]
    num = jnp.stack(
        [
            num1[..., i, :, :] * f1[..., i : i + 1, :] + num2[..., i, :, :] * f2[..., i : i + 1, :]
            for i in range(heads)
        ],
        axis=-3,
    )
    return [num, jnp.concatenate([highest, sum1 * f1 + sum2 * f2], axis=-2)]


def loop(count, step):
    if count == 1:
        step(0)
    else:
        lax.fori_loop(0, count, lambda i, carry: (step(i), carry)[1], 0)


def combine_down(grid, me, reqs, join, ps, sc, sems, produce=None):
    R, A, B = reqs, grid.size["a"], grid.size["b"]
    r, a, b, c = (me["r"] if R > 1 else 0), me["a"], me["b"], me["c"]
    n = len(ps)
    parts = range(n)
    base_r = R * B * A * n
    base_b = base_r + (R - 1) * B * A * n
    base_a = base_b + (B - 1) * A * n
    db_order = list(range(1, B)) + [0]
    dr_order = list(range(1, R)) + [0]

    def where(dr, db, i):
        rr = (r + dr) % R if dr else r
        bb = (b + db) % B if db else b
        return rr, (a + i + 1) % A, bb

    def copies(base, pairs, device):
        return [
            remote(src, dst, sems.at[0, base + k], sems.at[1, base + k], device)
            for k, (src, dst) in enumerate(pairs)
        ]

    def core(dr, db, i):
        rr, aa, bb = where(dr, db, i)
        return copies(
            ((dr * B + db) * A + i) * n,
            [(ps[k].at[rr, aa, bb, 1 - c], sc["r1"][k].at[dr, db, i]) for k in parts],
            grid.device(grid.moved(me, c=1)),
        )

    def along_r(dr, db, i):
        return copies(
            base_r + (((dr - 1) * B + db) * A + i) * n,
            [(sc["t1"][k].at[dr - 1, db, i], sc["r2"][k].at[dr - 1, db, i]) for k in parts],
            grid.device(grid.moved(me, r=dr)),
        )

    def along_b(db, i):
        return copies(
            base_b + ((db - 1) * A + i) * n,
            [(sc["t2"][k].at[db - 1, i], sc["r3"][k].at[db - 1, i]) for k in parts],
            grid.device(grid.moved(me, b=db)),
        )

    def along_a(da):
        return copies(
            base_a + (da - 1) * n,
            [(sc["t3"][k].at[da - 1], sc["r4"][k].at[da - 1]) for k in parts],
            grid.device(dict(me, a=(a + da) % A)),
        )

    def start(made):
        for copy in made:
            copy.start()

    def arrived(made):
        for copy in made:
            copy.wait_recv()

    def wide_values(refs):
        return [ref[...].astype(jnp.float32) for ref in refs]

    def at_chip(dr, db, i):
        rr, aa, bb = where(dr, db, i)
        arrived(core(dr, db, i))
        both = join(
            wide_values([ps[k].at[rr, aa, bb, c] for k in parts]),
            wide_values([sc["r1"][k].at[dr, db, i] for k in parts]),
        )
        if dr == 0:
            for step in range(1, R):
                arrived(along_r(step, db, i))
                both = join(both, wide_values([sc["r2"][k].at[step - 1, db, i] for k in parts]))
        return both

    def keep(name, at, values):
        for k in parts:
            sc[name][k][at] = values[k].astype(sc[name][k].dtype)

    def to_r(dr, db, i):
        keep("t1", (dr - 1, db, i), at_chip(dr, db, i))
        start(along_r(dr, db, i))

    def to_b(db, i):
        keep("t2", (db - 1, i), at_chip(0, db, i))
        start(along_b(db, i))

    def on_b(i):
        both = at_chip(0, 0, i)
        for db in range(1, B):
            arrived(along_b(db, i))
            both = join(both, wide_values([sc["r3"][k].at[db - 1, i] for k in parts]))
        return both

    def to_a(i):
        keep("t3", (i,), on_b(i))
        start(along_a(i + 1))

    if produce is None:
        for dr in dr_order:
            for db in db_order:
                loop(A, lambda i: start(core(dr, db, i)))
        for dr in range(1, R):
            for db in db_order:
                loop(A, lambda i: to_r(dr, db, i))
        for db in range(1, B):
            loop(A, lambda i: to_b(db, i))
    else:
        before = None
        for db in db_order:

            def step(i):
                produce(where(0, db, i))
                start(core(0, db, i))
                if before:
                    pl.when(i == 0)(lambda: to_b(before, A - 1))
                if db:
                    pl.when(i > 0)(lambda: to_b(db, i - 1))

            lax.fori_loop(0, A, lambda i, carry: (step(i), carry)[1], 0)
            before = db
    if A > 1:
        loop(A - 1, to_a)
    total = on_b(A - 1)
    for da in range(1, A):
        arrived(along_a(da))
        total = join(total, wide_values([sc["r4"][k].at[da - 1] for k in parts]))

    def finish():
        def sent(made):
            for copy in made:
                copy.wait_send()

        for dr in range(R):
            for db in range(B):
                loop(A, lambda i: sent(core(dr, db, i)))
                if dr:
                    loop(A, lambda i: sent(along_r(dr, db, i)))
        for db in range(1, B):
            loop(A, lambda i: sent(along_b(db, i)))
        for da in range(1, A):
            sent(along_a(da))

    return total, finish


SCRATCH = ("r1", "t1", "r2", "t2", "r3", "t3", "r4")


def reduce_scratch(grid, reqs, slabs):
    R, A, B = reqs, grid.size["a"], grid.size["b"]
    lead = dict(
        r1=(R, B, A),
        t1=(R - 1, B, A) if R > 1 else (1, 1, 1),
        r2=(R - 1, B, A) if R > 1 else (1, 1, 1),
        t2=(max(B - 1, 1), A),
        r3=(max(B - 1, 1), A),
        t3=(max(A - 1, 1),),
        r4=(max(A - 1, 1),),
    )
    shapes = [
        pltpu.VMEM(lead[name] + tuple(shape), dtype) for name in SCRATCH for shape, dtype in slabs
    ]
    count = (R * B * A + (R - 1) * B * A + (B - 1) * A + (A - 1)) * len(slabs)
    shapes.append(pltpu.SemaphoreType.DMA((2, count)))
    return shapes


def reduce_kernel(grid, reqs, p_ref, o_ref, *rest):
    sems = rest[-1]
    sc = {name: [rest[k]] for k, name in enumerate(SCRATCH)}
    me = grid.place()
    grid.barrier(me, ("r", "a", "b", "c"))
    (total,), finish = combine_down(grid, me, reqs, add_join, [p_ref], sc, sems)
    o_ref[...] = total.astype(o_ref.dtype)
    finish()


def reduce_scatter(grid, reqs, x, out_dtype, collective_id):
    slab = x.shape[1:]
    vmem = pl.BlockSpec(memory_space=pltpu.VMEM)
    return pl.pallas_call(
        functools.partial(reduce_kernel, grid, reqs),
        out_shape=jax.ShapeDtypeStruct(slab, out_dtype),
        in_specs=[vmem],
        out_specs=vmem,
        scratch_shapes=reduce_scratch(grid, reqs, [(slab, x.dtype)]),
        compiler_params=params(collective_id),
        name="reduce" + str(collective_id),
    )(x.reshape((reqs, grid.size["a"], grid.size["b"], 2) + slab))


def cache_kernel(
    grid, heads, q_ref, k_hbm, v_hbm, ok_ref, num_out, st_out, k_ref, v_ref, num, st, loads, *rest
):
    sems = rest[-1]
    sc = {name: rest[2 * k : 2 * k + 2] for k, name in enumerate(SCRATCH)}
    me = grid.place()
    B = grid.size["b"]
    groups = HEADS // GROUP
    slabs = GROUP // heads

    def load(g):
        cols = pl.ds(pl.multiple_of(g * GROUP * HD, GROUP * HD), GROUP * HD)
        return [
            pltpu.make_async_copy(hbm.at[0, :, cols], ref.at[g], loads.at[k, g])
            for k, (hbm, ref) in enumerate(((k_hbm, k_ref), (v_hbm, v_ref)))
        ]

    def group(g):
        for copy in load(g):
            copy.wait()
        ok = ok_ref[...] > 0.0
        for j in range(slabs):
            slab = g * slabs + j
            at = (0, slab // (2 * B), (slab // 2) % B, slab % 2)
            tops, sums = [], []
            for h in range(heads):
                lanes = slice((j * heads + h) * HD, (j * heads + h + 1) * HD)
                scores = jnp.dot(
                    k_ref[g, :, lanes], q_ref[slab, h], preferred_element_type=jnp.float32
                ) * HD ** (-0.5)
                scores = jnp.where(ok, scores, NEG_LARGE)
                top = jnp.max(scores, axis=0, keepdims=True)
                weights = jnp.where(ok, jnp.exp(scores - top), 0.0)
                num[at + (h,)] = lax.dot_general(
                    v_ref[g, :, lanes],
                    weights.astype(jnp.bfloat16),
                    (((0,), (0,)), ((), ())),
                    preferred_element_type=jnp.float32,
                ).astype(jnp.bfloat16)
                tops.append(top)
                sums.append(jnp.sum(weights, axis=0, keepdims=True))
            blank = [jnp.zeros((GROUP - heads, SPAN), jnp.float32)]
            st[at] = jnp.concatenate(tops + blank + sums + blank, axis=0)

    loop(groups, lambda g: [copy.start() for copy in load(g)] and None)
    grid.barrier(me, ("a", "b", "c"))
    if slabs == 2:
        produce = lambda place: group(place[1] * B + place[2])
    else:
        loop(groups, group)
        produce = None
    total, finish = combine_down(grid, me, 1, softmax_join, [num, st], sc, sems, produce)
    num_out[...] = total[0]
    st_out[...] = total[1]
    finish()


def cache_attention(grid, heads, query, keys, values, usable, collective_id):
    block = keys.shape[1]
    groups = HEADS // GROUP
    lead = (1, grid.size["a"], grid.size["b"], 2)
    num = ((heads, HD, SPAN), jnp.bfloat16)
    stats = ((2 * GROUP, SPAN), jnp.float32)
    vmem = pl.BlockSpec(memory_space=pltpu.VMEM)
    hbm = pl.BlockSpec(memory_space=pl.ANY)
    return pl.pallas_call(
        functools.partial(cache_kernel, grid, heads),
        in_specs=[vmem, hbm, hbm, vmem],
        out_specs=[vmem, vmem],
        out_shape=[
            jax.ShapeDtypeStruct(num[0], jnp.float32),
            jax.ShapeDtypeStruct(stats[0], jnp.float32),
        ],
        scratch_shapes=[
            pltpu.VMEM((groups, block, GROUP * HD), jnp.bfloat16),
            pltpu.VMEM((groups, block, GROUP * HD), jnp.bfloat16),
            pltpu.VMEM(lead + num[0], num[1]),
            pltpu.VMEM(lead + stats[0], stats[1]),
            pltpu.SemaphoreType.DMA((2, groups)),
        ]
        + reduce_scratch(grid, 1, [num, stats]),
        compiler_params=params(collective_id),
        name="cache_attention",
    )(query, keys, values, usable)


def middle_kernel(grid, p_ref, gain_ref, o_ref, mid_ref, *rest):
    scratch, sems, send, recv, local = rest[:-4], rest[-4], rest[-3], rest[-2], rest[-1]
    sc = {name: [scratch[k]] for k, name in enumerate(SCRATCH)}
    me = grid.place()
    grid.barrier(me, ("r", "a", "b", "c"))
    (total,), finish = combine_down(grid, me, 1, add_join, [p_ref], sc, sems)
    meansq = jnp.mean(total * total, axis=-1, keepdims=True)
    scaled = total * lax.rsqrt(meansq + EPSILON) * gain_ref[...].astype(jnp.float32)
    mid_ref[...] = scaled.astype(mid_ref.dtype)
    spread(grid, me, ("a", "b", "r", "c"), mid_ref, o_ref, send, recv, local)
    finish()


def middle(grid, part, gain, collective_id):
    slots = grid.size["r"] * grid.wide
    slab = part.shape[1:]
    vmem = pl.BlockSpec(memory_space=pltpu.VMEM)
    return pl.pallas_call(
        functools.partial(middle_kernel, grid),
        out_shape=jax.ShapeDtypeStruct((slots,) + slab, jnp.bfloat16),
        in_specs=[vmem, vmem],
        out_specs=vmem,
        scratch_shapes=[pltpu.VMEM(slab, jnp.bfloat16)]
        + reduce_scratch(grid, 1, [(slab, jnp.bfloat16)])
        + [
            pltpu.SemaphoreType.DMA((2 * slots + 2,)),
            pltpu.SemaphoreType.DMA((slots,)),
            pltpu.SemaphoreType.DMA,
        ],
        compiler_params=params(collective_id),
        name="middle",
    )(part.reshape((1, grid.size["a"], grid.size["b"], 2) + slab), gain.reshape(1, -1))


def body(
    grid,
    tokens,
    attn_gain,
    qkv_weight,
    adapter_down,
    adapter_up,
    out_weight,
    mlp_gain,
    gate_up,
    down_weight,
    key_cache,
    value_cache,
    cache_lengths,
    slot_mask,
    span_counts,
):
    reqs, wide = grid.size["r"], grid.wide
    rows = tokens.shape[0]
    width = qkv_weight.shape[2]
    heads = width // HD
    wide_index = lax.axis_index("wide")
    query_all, query_turned, keys_turned, values_turned = project(
        grid, tokens, attn_gain, qkv_weight, adapter_down, adapter_up, 0
    )
    new_keys = keys_turned.T
    new_values = values_turned.T
    query_all = query_all.reshape(wide, heads, HD, SPAN)
    query_turned = query_turned.reshape(heads, HD, SPAN)

    block_len = key_cache.shape[1]
    positions = wide_index * block_len + jnp.arange(block_len)
    usable = ((positions < cache_lengths[0]) & (slot_mask[0] == 1)).astype(jnp.float32)
    usable = jnp.broadcast_to(usable[:, None], (block_len, SPAN))
    cache_num, cache_stats = cache_attention(
        grid, heads, query_all, key_cache, value_cache, usable, 3
    )

    span_count = span_counts[0]
    query_pos = jnp.arange(SPAN)[None, :]
    key_pos = jnp.arange(SPAN)[:, None]
    span_ok = (key_pos <= query_pos) & ((key_pos < span_count) | (key_pos == query_pos))
    own_scores = (
        jnp.einsum(
            "hdq,khd->hkq",
            query_turned,
            new_keys.reshape(SPAN, heads, HD),
            preferred_element_type=jnp.float32,
        )
        * HD ** (-0.5)
    )
    own_scores = jnp.where(span_ok, own_scores, NEG_LARGE)
    own_max = jnp.max(own_scores, axis=1)
    own_weights = jnp.where(span_ok, jnp.exp(own_scores - own_max[:, None]), 0.0)
    own_sum = jnp.sum(own_weights, axis=1)
    own_num = jnp.einsum(
        "hkq,khd->hdq",
        own_weights.astype(jnp.bfloat16),
        new_values.reshape(SPAN, heads, HD),
        preferred_element_type=jnp.float32,
    )
    cache_max, cache_sum = cache_stats[:heads], cache_stats[GROUP : GROUP + heads]
    highest = jnp.maximum(cache_max, own_max)
    cache_factor = jnp.exp(cache_max - highest)
    own_factor = jnp.exp(own_max - highest)
    totals = cache_sum * cache_factor + own_sum * own_factor
    mixed = cache_num * cache_factor[:, None] + own_num * own_factor[:, None]
    attention = (mixed / totals[:, None]).astype(jnp.bfloat16).reshape(width, SPAN).T

    attn_part = jnp.dot(attention, out_weight, preferred_element_type=jnp.float32)
    every_row = middle(
        grid, attn_part.astype(jnp.bfloat16).reshape(wide, rows, -1), mlp_gain, 4
    ).reshape(reqs * SPAN, -1)
    both = jnp.einsum("td,cfd->ctf", every_row, gate_up, preferred_element_type=jnp.float32)
    hidden = (jax.nn.silu(both[0]) * both[1]).astype(jnp.bfloat16)
    mlp_part = jnp.dot(hidden, down_weight, preferred_element_type=jnp.float32)
    hidden_out = reduce_scatter(
        grid,
        reqs,
        mlp_part.astype(jnp.bfloat16).reshape(reqs * wide, rows, -1),
        jnp.bfloat16,
        6,
    )
    return (hidden_out, attention, new_keys, new_values)


def solution(mesh):
    grid = Grid(mesh.shape["req"], mesh.shape["wide"])
    return jax.shard_map(
        functools.partial(body, grid),
        mesh=mesh,
        in_specs=(
            P(("req", "wide"), None),
            P(),
            P(None, None, "wide"),
            P("wide", None),
            P(None, None, "wide"),
            P("wide", None),
            P(),
            P(None, ("req", "wide"), None),
            P(("req", "wide"), None),
            P("req", "wide", None),
            P("req", "wide", None),
            P("req"),
            P("req", "wide"),
            P("req"),
        ),
        out_specs=(P(("req", "wide"), None), P("req", "wide"), P("req", "wide"), P("req", "wide")),
        check_vma=False,
    )
```
